256 devices in a mesh: sec: 32 (over x, y, core), tp: 8 (over z).
Axes of the slice: x: 4, y: 4, z: 8, core: 2. Of those that a mesh axis runs over, the one named last changes fastest.
Arguments:
- encoded: bfloat16 [16384, 4096], P('sec', 'tp'), may hold values from -9 to 9
- decoder_states: bfloat16 [512, 4096], P(None, 'tp'), may hold values from -10 to 10
- passage_counts: int32 [8], replicated, may hold values from 1 to 16, 64 in all
- enc_gain: float32 [4096], replicated, may hold values from 0.25 to 1.75
- dec_gain: float32 [4096], replicated, may hold values from 0.25 to 1.75
- w_key: bfloat16 [4096, 4096], P('sec', 'tp'), may hold values from -1 to 1
- w_value: bfloat16 [4096, 4096], P('sec', 'tp'), may hold values from -0.09375 to 0.09375
- w_query: bfloat16 [4096, 4096], P('sec', 'tp'), may hold values from -1 to 1
- w_out: bfloat16 [4096, 4096], P('tp', 'sec'), may hold values from -0.09375 to 0.09375
Outputs:
- decoded: bfloat16 [512, 4096], P(None, 'tp')
- passage_scores: float32 [64], P('sec')
The draws below stay inside these ranges and needn't reach their ends.
Inputs may be any that keep to these rules, and one draw needn't show every extreme that they name: `passage_counts`: every question has at least one passage; the counts sum to 64, the largest is exactly 16.
All inputs are finite; a program needn't handle non-finite values.
Results may differ from the reference program's by a relative error of at most 0.015.
Values may be sent and summed in bfloat16 or wider, within the bound.
No kernel may reach another device: no remote copies, remote signals or barrier semaphores. Data moves between devices by JAX's collectives and lax.ppermute only.
A program may use at most 128 MiB of HBM per device.

```python
import math
import jax
import jax.numpy as jnp
import numpy as np
from jax import lax

D = 4096
HEADS = 64
HEAD_DIM = 64
PTOK = 256
QUESTIONS = 8
QTOK = 64
INNER = 4096
SLOTS = 64
QROWS = 512
N_TP = 8


aligned_strength = 18.0


def shared_signs(key):
    first, second, third = jax.random.split(key, 3)
    query_dir = (2 * jax.random.randint(first, (D,), 0, 2) - 1).astype(jnp.float32)
    key_dir = (2 * jax.random.randint(second, (D,), 0, 2) - 1).astype(jnp.float32)
    head_dir = (2 * jax.random.randint(third, (INNER,), 0, 2) - 1).astype(jnp.float32)
    return (query_dir, key_dir, head_dir)


def draw_decoder_states(key, part):
    query_dir, key_dir, head_dir = shared_signs(key)
    key = jax.random.fold_in(key, 3)
    noise_key, level_key = jax.random.split(key)
    noise = jnp.clip(jax.random.normal(noise_key, (QROWS, D), jnp.float32), -6.0, 6.0)
    level = jax.random.randint(level_key, (QROWS, 1), 0, 32)
    strength = jnp.where(level == 0, 0.5, jnp.where(level == 1, 1.0, jnp.where(level == 2, 2.0, jnp.where(level == 3, 4.0, 0.0))))
    return (noise + strength * query_dir[None, :]).astype(jnp.bfloat16)


def draw_encoded(key, part):
    query_dir, key_dir, head_dir = shared_signs(key)
    key = jax.random.fold_in(key, 5)
    noise_key, level_key = jax.random.split(key)
    noise = jnp.clip(jax.random.normal(noise_key, (SLOTS * PTOK, D), jnp.float32), -6.0, 6.0)
    level = jax.random.randint(level_key, (SLOTS * PTOK, 1), 0, 32)
    strength = jnp.where(level == 0, 2.0, jnp.where(level == 1, 3.0, 0.0))
    return (noise + strength * key_dir[None, :]).astype(jnp.bfloat16)


def draw_w_query(key, part):
    query_dir, key_dir, head_dir = shared_signs(key)
    key = jax.random.fold_in(key, 7)
    base = jnp.clip(jax.random.normal(key, (D, INNER), jnp.float32), -6.0, 6.0)
    planted = aligned_strength / (D * HEAD_DIM ** 0.5) * query_dir[:, None] * head_dir[None, :]
    return (base * D ** (-0.5) + planted).astype(jnp.bfloat16)


def draw_w_key(key, part):
    query_dir, key_dir, head_dir = shared_signs(key)
    key = jax.random.fold_in(key, 9)
    base = jnp.clip(jax.random.normal(key, (D, INNER), jnp.float32), -6.0, 6.0)
    planted = aligned_strength / (D * HEAD_DIM ** 0.5) * key_dir[:, None] * head_dir[None, :]
    return (base * D ** (-0.5) + planted).astype(jnp.bfloat16)


def shard_levels(own_key, extent, cuts, least, high):
    loudness, own = 1.0, jax.random.fold_in(own_key, 6)
    for axis_at, parts in cuts:
        steps = jnp.exp(jax.random.uniform(jax.random.fold_in(own, axis_at), (parts,), jnp.float32, least / len(cuts), high / len(cuts)))
        loudness = loudness * jnp.repeat(steps, extent[axis_at] // parts).reshape([-1 if axis == axis_at else 1 for axis in range(len(extent))])
    return loudness


def length_profile(number_of, total, bound, slope):
    portions = [(1 << 20) // math.isqrt(rank ** slope) + 1 for rank in range(2, number_of + 1)]
    spare, counts = total - bound - (number_of - 1), [1] * (number_of - 1)
    while spare > 0:
        free = [i for i in range(number_of - 1) if counts[i] < bound]
        whole, budget = sum([portions[i] for i in free]), spare
        for i in free:
            more = min(bound - counts[i], max(1, budget * portions[i] // whole), spare)
            counts[i] = counts[i] + more
            spare = spare - more
    return np.array([bound] + counts)


def uneven_parts(rng, number_of, total, reach, lean):
    if number_of == 2:
        one = jax.random.randint(rng, (), max(1, total - reach), min(reach, total - 1) + 1)
        return jnp.stack([one, total - one])
    lengths = jnp.asarray(length_profile(number_of, total, reach, lean), jnp.int32)
    couples = (number_of - 1) // 2
    source_of, taker = lengths[1:1 + 2 * couples:2], lengths[2:2 + 2 * couples:2]
    margin = jnp.minimum(source_of - 1, reach - taker)
    shifted = jax.random.randint(jax.random.fold_in(rng, 1), (couples,), 0, 1 << 20) % (margin + 1)
    lengths = lengths.at[1:1 + 2 * couples:2].set(source_of - shifted).at[2:2 + 2 * couples:2].set(taker + shifted)
    return lengths[jax.random.permutation(jax.random.fold_in(rng, 2), number_of)]


def bell_draw(key, dims, spread, reach, cuts=(), kind=jnp.bfloat16):
    drawn = spread * jax.random.normal(key, dims, jnp.float32)
    if cuts:
        drawn = drawn * shard_levels(key, dims, cuts, -0.22, 0.18)
    return jnp.clip(drawn, -reach, reach).astype(kind)


def setup_inputs(seed: int = 0) -> dict:
    key_list = jax.random.split(jax.random.key(seed), 10)
    return {
        "encoded": draw_encoded(jax.random.fold_in(key_list[9], 71), 0),
        "decoder_states": draw_decoder_states(jax.random.fold_in(key_list[9], 71), 0),
        "passage_counts": uneven_parts(key_list[2], QUESTIONS, SLOTS, SLOTS // 4, 2).astype(jnp.int32),
        "enc_gain": jnp.clip(1.0 + 0.15 * jax.random.normal(key_list[3], (D,), jnp.float32), 0.25, 1.75),
        "dec_gain": jnp.clip(1.0 + 0.15 * jax.random.normal(key_list[4], (D,), jnp.float32), 0.25, 1.75),
        "w_key": draw_w_key(jax.random.fold_in(key_list[9], 71), 0),
        "w_value": bell_draw(key_list[6], (D, INNER), D ** -0.5, 0.09375, ((0, 32), (1, 8))),
        "w_query": draw_w_query(jax.random.fold_in(key_list[9], 71), 0),
        "w_out": bell_draw(key_list[8], (INNER, D), INNER ** -0.5, 0.09375, ((0, 8), (1, 32))),
    }


def rms_norm(states, gain):
    values = states.astype(jnp.float32)
    scale = lax.rsqrt(lax.optimization_barrier(jnp.mean(values * values, axis=-1, keepdims=True)) + 1e-06)
    return (values * scale * gain).astype(jnp.bfloat16)

def reference(encoded, decoder_states, passage_counts, enc_gain, dec_gain, w_key, w_value, w_query, w_out):
    enc_normed = rms_norm(encoded, enc_gain)
    keys = jnp.dot(enc_normed, w_key, preferred_element_type=jnp.float32).astype(jnp.bfloat16)
    values = jnp.dot(enc_normed, w_value, preferred_element_type=jnp.float32).astype(jnp.bfloat16)
    dec_normed = rms_norm(decoder_states, dec_gain)
    queries = jnp.dot(dec_normed, w_query, preferred_element_type=jnp.float32).astype(jnp.bfloat16)
    ends = jnp.cumsum(passage_counts).astype(jnp.int32)
    slot_ids = jnp.arange(SLOTS, dtype=jnp.int32)
    slot_owner = lax.optimization_barrier(jnp.sum((slot_ids[:, None] >= ends[None, :]).astype(jnp.int32), axis=1))
    key_owner = jnp.repeat(slot_owner, PTOK)
    query_owner = jnp.arange(QROWS, dtype=jnp.int32) // QTOK
    mask = query_owner[:, None] == key_owner[None, :]
    head_queries = queries.reshape(QROWS, HEADS, HEAD_DIM).transpose(1, 0, 2)
    head_keys = keys.reshape(SLOTS * PTOK, HEADS, HEAD_DIM).transpose(1, 0, 2)
    head_values = values.reshape(SLOTS * PTOK, HEADS, HEAD_DIM).transpose(1, 0, 2)

    def one_head(operands):
        query_h, key_h, value_h = operands
        scores = jnp.dot(query_h, key_h.T, preferred_element_type=jnp.float32)
        scores = jnp.where(mask, scores, jnp.float32(-1e+30))
        top = lax.optimization_barrier(jnp.max(scores, axis=1, keepdims=True))
        weights = jnp.where(mask, jnp.exp(scores - top), jnp.float32(0.0))
        total = lax.optimization_barrier(jnp.sum(weights, axis=1, keepdims=True))
        context = jnp.dot(weights.astype(jnp.bfloat16), value_h, preferred_element_type=jnp.float32) / total
        pooled = lax.optimization_barrier(jnp.sum((weights / total).reshape(QROWS, SLOTS, PTOK), axis=(0, 2)))
        return (context.astype(jnp.bfloat16), pooled)
    contexts, pooled = lax.map(one_head, (head_queries, head_keys, head_values))
    context = contexts.transpose(1, 0, 2).reshape(QROWS, INNER)
    group = INNER // N_TP
    cross = jnp.zeros((QROWS, D), jnp.float32)
    for index in range(N_TP):
        partial_sum = jnp.dot(context[:, index * group:(index + 1) * group], w_out[index * group:(index + 1) * group, :], preferred_element_type=jnp.float32)
        cross = cross + partial_sum.astype(jnp.bfloat16).astype(jnp.float32)
    decoded = (decoder_states.astype(jnp.float32) + cross).astype(jnp.bfloat16)
    passage_scores = lax.optimization_barrier(jnp.sum(pooled, axis=0)) / (HEADS * QTOK)
    return (decoded, passage_scores)
```

```python
import jax
import jax.numpy as jnp
from jax import lax
from jax.experimental import pallas as pl
from jax.experimental.pallas import tpu as pltpu
from jax.sharding import PartitionSpec as P

HEADS = 64
HEAD_DIM = 64
PTOK = 256
QTOK = 64
SIDE = 4
CORES = 2
ABSENT = -1e30
BF16 = jnp.bfloat16
F32 = jnp.float32
REACH = (0, -1, 1, 2)


def sec_id(x, y, c):
    return ((x % SIDE) * SIDE + y % SIDE) * CORES + c


def along_tp(v, step):
    n = lax.axis_size("tp")
    return lax.ppermute(v, "tp", [(i, (i + step) % n) for i in range(n)])


def along_tp_by_core(v):
    n = lax.axis_size("tp")
    s = lax.axis_size("sec")
    pairs = [
        (i * n + z, i * n + (z + (1 if i % CORES == 0 else -1)) % n)
        for i in range(s)
        for z in range(n)
    ]
    return lax.ppermute(v, ("sec", "tp"), pairs)


def other_core(v):
    s = lax.axis_size("sec")
    return lax.ppermute(v, "sec", [(i, i ^ 1) for i in range(s)])


def in_plane(v, step, swap):
    pairs = []
    for x in range(SIDE):
        for y in range(SIDE):
            for c in range(CORES):
                on_x = (c == 0) != swap
                to = sec_id(x + step, y, c) if on_x else sec_id(x, y + step, c)
                pairs.append((sec_id(x, y, c), to))
    return lax.ppermute(v, "sec", pairs)


def ring_gather(piece):
    core = lax.axis_index("sec") % CORES
    up = down = piece
    held = [piece]
    for _ in range(3):
        up, down = along_tp(up, 1), along_tp(down, -1)
        held += [up, down]
    held.append(along_tp_by_core(jnp.where(core == 0, up, down)))
    return held


def plane_gather(shard):
    half = shard.shape[0] // 2
    a, b = in_plane(shard, 1, False), in_plane(shard, -1, False)
    c, d = in_plane(a[:half], 1, False), in_plane(b[half:], -1, False)
    g = jnp.concatenate([shard, a, b, c, d], 0)
    ga, gb = in_plane(g, 1, True), in_plane(g, -1, True)
    half = g.shape[0] // 2
    gc, gd = in_plane(ga[:half], 1, True), in_plane(gb[half:], -1, True)
    own = [g, ga, gb, gc, gd]
    return own + [other_core(v) for v in own]


def high_low(v):
    high = v.astype(BF16).astype(F32)
    return high, (v - high).astype(BF16).astype(F32)


def attend_kernel(
    info, gains, *refs
):
    x_parts, w_parts = refs[:8], refs[8:18]
    out, wo = refs[18:20]
    xs, ws, ks, vs, qs, scale, sems = refs[20:]
    sec, tp, first, own_a, own_b = info[0], info[1], info[2], info[3], info[4]
    core = sec % CORES
    px = sec // (SIDE * CORES)
    py = (sec // CORES) % SIDE
    for part, off in zip(x_parts, (0, -1, 1, -2, 2, -3, 3, 4)):
        at = pl.multiple_of(((tp + off + 8) % 8) * 512, 512)
        pltpu.make_async_copy(part, xs.at[:, pl.ds(at, 512)], sems.at[0]).start()
    shards = []
    for mine in (True, False):
        group = w_parts[:5] if mine else w_parts[5:]
        col = core if mine else 1 - core
        for r2 in REACH:
            for at, r1 in enumerate(REACH):
                if r2 == 2:
                    ref, row = (group[3], at) if at < 2 else (group[4], at - 2)
                else:
                    ref, row = group[REACH.index(r2)], at
                dx = jnp.where(col == 0, r1, r2)
                dy = jnp.where(col == 0, r2, r1)
                s = (((px + dx + SIDE) % SIDE) * SIDE + (py + dy + SIDE) % SIDE) * CORES + col
                shards.append((ref, row, s))
    for ref, row, s in shards:
        pltpu.make_async_copy(ref.at[pl.ds(row * 512, 384)], ws.at[s], sems.at[1]).start()
    for ref, row, s in shards:
        pltpu.make_async_copy(
            ref.at[pl.ds(row * 512 + 384, 128)],
            wo.at[pl.ds(pl.multiple_of(s * 128, 128), 128)],
            sems.at[2],
        ).start()

    lane = lax.broadcasted_iota(jnp.int32, (1, 128), 1)
    rest = jnp.where(lane < 8, ABSENT, 0.0)
    out[:, :512] = jnp.zeros((512, 512), BF16)
    out[:, 512:] = jnp.broadcast_to(rest, (512, 128)).astype(BF16)

    pltpu.make_async_copy(xs, xs, sems.at[0]).wait()

    @pl.loop(0, 5)
    def _(i):
        rows = pl.ds(pl.multiple_of(i * 128, 128), 128)
        which = pl.ds((i == 4).astype(jnp.int32), 1)
        total = jnp.zeros((128, 1), F32)
        for j in range(8):
            cols = slice(512 * j, 512 * (j + 1))
            v = xs[rows, cols].astype(F32)
            total = total + jnp.sum(v * v, axis=1, keepdims=True)
            xs[rows, cols] = (v * gains[which, cols]).astype(BF16)
        scale[rows, :] = jnp.broadcast_to(lax.rsqrt(total / 4096.0 + 1e-06), (128, 128))

    pltpu.make_async_copy(ws, ws, sems.at[1]).wait()

    @pl.loop(0, 2)
    def _(n):
        cols = pl.ds(pl.multiple_of(n * 256, 256), 256)
        wq = ws[:, 256:384, cols].reshape(4096, 256)
        q = jnp.dot(xs[512:640, :], wq, preferred_element_type=F32)
        qs[:, cols] = (q * scale[512:640, 0:1]).astype(BF16)
        wk = ws[:, 0:128, cols].reshape(4096, 256)
        k = jnp.dot(xs[0:512, :], wk, preferred_element_type=F32)
        ks[:, cols] = (k * scale[0:512, 0:1]).astype(BF16)
        wv = ws[:, 128:256, cols].reshape(4096, 256)
        v = jnp.dot(xs[0:512, :], wv, preferred_element_type=F32)
        vs[:, cols] = (v * scale[0:512, 0:1]).astype(BF16)

    row_owner = first + lax.broadcasted_iota(jnp.int32, (128, 512), 0) // QTOK
    key_owner = jnp.where(lax.broadcasted_iota(jnp.int32, (128, 512), 1) < PTOK, own_a, own_b)
    keep = row_owner == key_owner
    window = pl.ds(pl.multiple_of(first * QTOK, QTOK), 128)
    lane = lax.broadcasted_iota(jnp.int32, (128, 128), 1)
    stats = jnp.zeros((128, 128), F32)
    for pair in range(4):
        cols = slice(128 * pair, 128 * (pair + 1))
        q2, k2, v2 = qs[:, cols], ks[:, cols], vs[:, cols]
        sums = []
        for side in range(2):
            h = 2 * pair + side
            mine = (lane < 64) if side == 0 else (lane >= 64)
            qh = jnp.where(mine, q2.astype(F32), 0.0).astype(BF16)
            scores = lax.dot_general(qh, k2, (((1,), (1,)), ((), ())), preferred_element_type=F32)
            scores = jnp.where(keep, scores, ABSENT)
            top_hi, top_lo = high_low(jnp.max(scores, axis=1, keepdims=True))
            weights = jnp.where(keep, jnp.exp(scores - (top_hi + top_lo)), 0.0)
            a_hi, a_lo = high_low(jnp.sum(weights[:, :PTOK], axis=1, keepdims=True))
            b_hi, b_lo = high_low(jnp.sum(weights[:, PTOK:], axis=1, keepdims=True))
            for at, value in enumerate((top_hi, top_lo, a_hi, a_lo, b_hi, b_lo)):
                stats = jnp.where(lane == 8 * at + h, value, stats)
            sums.append(jnp.dot(weights.astype(BF16), v2, preferred_element_type=F32))
        out[window, cols] = jnp.where(lane < 64, sums[0], sums[1]).astype(BF16)
    out[window, 512:640] = stats.astype(BF16)
    pltpu.make_async_copy(wo, wo, sems.at[2]).wait()


def attend(info, gains, x_parts, w_parts):
    anywhere = pl.BlockSpec(memory_space=pl.ANY)
    inside = pl.BlockSpec(memory_space=pltpu.VMEM)
    return pl.pallas_call(
        attend_kernel,
        in_specs=[pl.BlockSpec(memory_space=pltpu.SMEM), inside] + [anywhere] * 18,
        out_specs=[inside, anywhere],
        out_shape=[
            jax.ShapeDtypeStruct((512, 640), BF16),
            jax.ShapeDtypeStruct((4096, 512), BF16),
        ],
        scratch_shapes=[
            pltpu.VMEM((640, 4096), BF16),
            pltpu.VMEM((32, 384, 512), BF16),
            pltpu.VMEM((512, 512), BF16),
            pltpu.VMEM((512, 512), BF16),
            pltpu.VMEM((128, 512), BF16),
            pltpu.VMEM((640, 128), F32),
            pltpu.SemaphoreType.DMA((3,)),
        ],
        compiler_params=pltpu.CompilerParams(vmem_limit_bytes=40 * 2**20),
        cost_estimate=pl.CostEstimate(
            flops=5 * 10**9, bytes_accessed=30 * 2**20, transcendentals=2**19
        ),
        name="project_attend",
    )(info, gains, *x_parts, *w_parts)


def merge_kernel(got, wo, out):
    st = got[:, 512:640].astype(F32)
    both = st + pltpu.roll(st, 120, 1)
    sum_a = pltpu.roll(both, 112, 1).reshape(32, 16, 128)
    sum_b = pltpu.roll(both, 96, 1).reshape(32, 16, 128)
    both = both.reshape(32, 16, 128)
    lane3 = lax.broadcasted_iota(jnp.int32, (32, 16, 128), 2)
    head = lane3 < 8
    tops = jnp.where(head, both, 0.0)
    top = jnp.max(tops, axis=0, keepdims=True)
    factor = jnp.exp(tops - top)
    sum_a = jnp.where(head, sum_a * factor, 0.0)
    sum_b = jnp.where(head, sum_b * factor, 0.0)
    total = jnp.sum(sum_a + sum_b, axis=0, keepdims=True)
    inverse = jnp.where(head[:1], 1.0 / total, 0.0)
    share_a = jnp.sum((sum_a * inverse).reshape(512, 128), axis=1, keepdims=True)
    share_b = jnp.sum((sum_b * inverse).reshape(512, 128), axis=1, keepdims=True)
    lane = lax.broadcasted_iota(jnp.int32, (512, 128), 1)
    slot = (lax.broadcasted_iota(jnp.int32, (512, 128), 0) // 16) * 2
    pooled = jnp.sum(
        jnp.where(lane == slot, share_a, 0.0) + jnp.where(lane == slot + 1, share_b, 0.0),
        axis=0,
        keepdims=True,
    )
    ratio_hi, ratio_lo = high_low((factor * inverse).reshape(512, 128))
    spread = (
        lax.broadcasted_iota(jnp.int32, (128, 512), 1) // HEAD_DIM
        == lax.broadcasted_iota(jnp.int32, (128, 512), 0)
    )
    spread = jnp.where(spread, 1.0, 0.0).astype(BF16)
    ratio = jnp.dot(ratio_hi.astype(BF16), spread, preferred_element_type=F32) + jnp.dot(
        ratio_lo.astype(BF16), spread, preferred_element_type=F32
    )
    context = jnp.sum((got[:, 0:512].astype(F32) * ratio).reshape(32, 16, 512), axis=0)
    context = context.astype(BF16)
    pool_hi, pool_lo = high_low(pooled)
    row = lax.broadcasted_iota(jnp.int32, (16, 128), 0)
    extra = jnp.where(row == 0, pool_hi, jnp.where(row == 1, pool_lo, 0.0)).astype(BF16)
    for z in range(8):
        term = lax.dot_general(
            context,
            wo[512 * z : 512 * (z + 1), :],
            (((1,), (1,)), ((), ())),
            preferred_element_type=F32,
        )
        out[z, :, 0:512] = term.astype(BF16)
        out[z, :, 512:640] = extra


def merge(got, wo):
    return pl.pallas_call(
        merge_kernel,
        out_shape=jax.ShapeDtypeStruct((8, 16, 640), BF16),
        compiler_params=pltpu.CompilerParams(vmem_limit_bytes=40 * 2**20),
        name="merge_project",
    )(got, wo)


def add_kernel(got, rows, out):
    sums = jnp.sum(got[...].astype(F32), axis=0)
    done = (rows[...].astype(F32) + sums[:, 0:512]).astype(BF16)
    pool_hi, pool_lo = high_low(jnp.sum(sums[:, 512:640], axis=0, keepdims=True))
    row = lax.broadcasted_iota(jnp.int32, (16, 128), 0)
    extra = jnp.where(row == 0, pool_hi, jnp.where(row == 1, pool_lo, 0.0)).astype(BF16)
    for s in range(32):
        out[s, :, 0:512] = done
        out[s, :, 512:640] = extra


def add_rows(got, rows):
    return pl.pallas_call(
        add_kernel,
        out_shape=jax.ShapeDtypeStruct((32, 16, 640), BF16),
        name="add_rows",
    )(got, rows)


def on_device(
    encoded, decoder_states, passage_counts, enc_gain, dec_gain, w_key, w_value, w_query, w_out
):
    sec = lax.axis_index("sec")
    tp = lax.axis_index("tp")
    questions = decoder_states.shape[0] // QTOK
    ends = jnp.cumsum(passage_counts)
    slots = sec * 2 + jnp.arange(2, dtype=jnp.int32)
    owner = jnp.sum((slots[:, None] >= ends[None, :]).astype(jnp.int32), axis=1)
    first = jnp.minimum(owner[0], questions - 2)
    info = jnp.stack([sec, tp, first, owner[0], owner[1]]).astype(jnp.int32)
    window = lax.dynamic_slice_in_dim(decoder_states, first * QTOK, 2 * QTOK, 0)
    x_parts = ring_gather(jnp.concatenate([encoded, window], 0))
    w_parts = plane_gather(jnp.concatenate([w_key, w_value, w_query, w_out.T], 0))
    gains = jnp.stack([enc_gain, dec_gain])
    partial, wo = attend(info, gains, x_parts, w_parts)
    got = lax.all_to_all(partial, "sec", 0, 0, tiled=True)
    terms = merge(got, wo)
    terms = lax.all_to_all(terms, "tp", 0, 0, tiled=True)
    rows = lax.dynamic_slice_in_dim(decoder_states, sec * 16, 16, 0)
    finished = lax.all_to_all(add_rows(terms, rows), "sec", 0, 0, tiled=True)
    decoded = finished[:, :, 0:512].reshape(512, 512)
    pooled = jnp.sum(finished[:, 0:2, 512:640].astype(F32), axis=(0, 1))
    passage_scores = lax.dynamic_slice_in_dim(pooled, sec * 2, 2, 0) / (HEADS * QTOK)
    return (decoded, passage_scores)


def solution(mesh):
    placed = (
        P("sec", "tp"),
        P(None, "tp"),
        P(),
        P(),
        P(),
        P("sec", "tp"),
        P("sec", "tp"),
        P("sec", "tp"),
        P("tp", "sec"),
    )
    return jax.shard_map(
        on_device, mesh=mesh, in_specs=placed, out_specs=(P(None, "tp"), P("sec")), check_vma=False
    )
```

```python
import jax
import jax.numpy as jnp
from jax import lax
from jax.experimental import pallas as pl
from jax.experimental.pallas import tpu as pltpu
from jax.sharding import PartitionSpec as P

HEADS = 64
HEAD_DIM = 64
PTOK = 256
QTOK = 64
SIDE = 4
CORES = 2
ABSENT = -1e30
BF16 = jnp.bfloat16
F32 = jnp.float32
REACH = (0, -1, 1, 2)


def sec_id(x, y, c):
    return ((x % SIDE) * SIDE + y % SIDE) * CORES + c


def along_tp(v, step):
    n = lax.axis_size("tp")
    return lax.ppermute(v, "tp", [(i, (i + step) % n) for i in range(n)])


def along_tp_by_core(v):
    n = lax.axis_size("tp")
    s = lax.axis_size("sec")
    pairs = [
        (i * n + z, i * n + (z + (1 if i % CORES == 0 else -1)) % n)
        for i in range(s)
        for z in range(n)
    ]
    return lax.ppermute(v, ("sec", "tp"), pairs)


def other_core(v):
    s = lax.axis_size("sec")
    return lax.ppermute(v, "sec", [(i, i ^ 1) for i in range(s)])


def in_plane(v, step, swap):
    pairs = []
    for x in range(SIDE):
        for y in range(SIDE):
            for c in range(CORES):
                on_x = (c == 0) != swap
                to = sec_id(x + step, y, c) if on_x else sec_id(x, y + step, c)
                pairs.append((sec_id(x, y, c), to))
    return lax.ppermute(v, "sec", pairs)


def ring_gather(piece):
    core = lax.axis_index("sec") % CORES
    up = down = piece
    held = [piece]
    for _ in range(3):
        up, down = along_tp(up, 1), along_tp(down, -1)
        held += [up, down]
    held.append(along_tp_by_core(jnp.where(core == 0, up, down)))
    return held


def plane_gather(shard):
    half = shard.shape[0] // 2
    a, b = in_plane(shard, 1, False), in_plane(shard, -1, False)
    c, d = in_plane(a[:half], 1, False), in_plane(b[half:], -1, False)
    g = jnp.concatenate([shard, a, b, c, d], 0)
    ga, gb = in_plane(g, 1, True), in_plane(g, -1, True)
    half = g.shape[0] // 2
    gc, gd = in_plane(ga[:half], 1, True), in_plane(gb[half:], -1, True)
    own = [g, ga, gb, gc, gd]
    return own + [other_core(v) for v in own]


def high_low(v):
    high = v.astype(BF16).astype(F32)
    return high, (v - high).astype(BF16).astype(F32)


def shard_places(w_parts, sec):
    core = sec % CORES
    px = sec // (SIDE * CORES)
    py = (sec // CORES) % SIDE
    shards = []
    for mine in (True, False):
        group = w_parts[:5] if mine else w_parts[5:]
        col = core if mine else 1 - core
        for r2 in REACH:
            for at, r1 in enumerate(REACH):
                if r2 == 2:
                    ref, row = (group[3], at) if at < 2 else (group[4], at - 2)
                else:
                    ref, row = group[REACH.index(r2)], at
                dx = jnp.where(col == 0, r1, r2)
                dy = jnp.where(col == 0, r2, r1)
                s = (((px + dx + SIDE) % SIDE) * SIDE + (py + dy + SIDE) % SIDE) * CORES + col
                shards.append((ref, row, s))
    return shards


def attend_kernel(info, gains, *refs):
    x_parts, w_parts = refs[:8], refs[8:18]
    out, xs, ws, ks, vs, qs, scale, sems = refs[18:]
    sec, tp, first, own_a, own_b = (info[i] for i in range(5))
    for part, off in zip(x_parts, (0, -1, 1, -2, 2, -3, 3, 4)):
        at = pl.multiple_of(((tp + off + 8) % 8) * 512, 512)
        pltpu.make_async_copy(part, xs.at[:, pl.ds(at, 512)], sems.at[0]).start()
    shards = shard_places(w_parts, sec)
    for ref, row, s in shards:
        pltpu.make_async_copy(ref.at[pl.ds(row * 512, 384)], ws.at[s], sems.at[1]).start()
    lane = lax.broadcasted_iota(jnp.int32, (1, 128), 1)
    rest = jnp.where(lane < 8, ABSENT, 0.0)
    out[:, :512] = jnp.zeros((512, 512), BF16)
    out[:, 512:] = jnp.broadcast_to(rest, (512, 128)).astype(BF16)

    pltpu.make_async_copy(xs, xs, sems.at[0]).wait()

    @pl.loop(0, 5)
    def _(i):
        rows = pl.ds(pl.multiple_of(i * 128, 128), 128)
        which = pl.ds((i == 4).astype(jnp.int32), 1)
        total = jnp.zeros((128, 1), F32)
        for j in range(8):
            cols = slice(512 * j, 512 * (j + 1))
            v = xs[rows, cols].astype(F32)
            total = total + jnp.sum(v * v, axis=1, keepdims=True)
            xs[rows, cols] = (v * gains[which, cols]).astype(BF16)
        scale[rows, :] = jnp.broadcast_to(lax.rsqrt(total / 4096.0 + 1e-06), (128, 128))

    pltpu.make_async_copy(ws, ws, sems.at[1]).wait()

    @pl.loop(0, 2)
    def _(n):
        cols = pl.ds(pl.multiple_of(n * 256, 256), 256)
        wq = ws[:, 256:384, cols].reshape(4096, 256)
        q = jnp.dot(xs[512:640, :], wq, preferred_element_type=F32)
        qs[:, cols] = (q * scale[512:640, 0:1]).astype(BF16)
        wk = ws[:, 0:128, cols].reshape(4096, 256)
        k = jnp.dot(xs[0:512, :], wk, preferred_element_type=F32)
        ks[:, cols] = (k * scale[0:512, 0:1]).astype(BF16)
        wv = ws[:, 128:256, cols].reshape(4096, 256)
        v = jnp.dot(xs[0:512, :], wv, preferred_element_type=F32)
        vs[:, cols] = (v * scale[0:512, 0:1]).astype(BF16)

    row_owner = first + lax.broadcasted_iota(jnp.int32, (128, 512), 0) // QTOK
    key_owner = jnp.where(lax.broadcasted_iota(jnp.int32, (128, 512), 1) < PTOK, own_a, own_b)
    keep = row_owner == key_owner
    window = pl.ds(pl.multiple_of(first * QTOK, QTOK), 128)
    lane = lax.broadcasted_iota(jnp.int32, (128, 128), 1)
    stats = jnp.zeros((128, 128), F32)
    for pair in range(4):
        cols = slice(128 * pair, 128 * (pair + 1))
        q2, k2, v2 = qs[:, cols], ks[:, cols], vs[:, cols]
        sums = []
        for side in range(2):
            h = 2 * pair + side
            mine = (lane < 64) if side == 0 else (lane >= 64)
            qh = jnp.where(mine, q2.astype(F32), 0.0).astype(BF16)
            scores = lax.dot_general(qh, k2, (((1,), (1,)), ((), ())), preferred_element_type=F32)
            scores = jnp.where(keep, scores, ABSENT)
            top_hi, top_lo = high_low(jnp.max(scores, axis=1, keepdims=True))
            weights = jnp.where(keep, jnp.exp(scores - (top_hi + top_lo)), 0.0)
            a_hi, a_lo = high_low(jnp.sum(weights[:, :PTOK], axis=1, keepdims=True))
            b_hi, b_lo = high_low(jnp.sum(weights[:, PTOK:], axis=1, keepdims=True))
            for at, value in enumerate((top_hi, top_lo, a_hi, a_lo, b_hi, b_lo)):
                stats = jnp.where(lane == 8 * at + h, value, stats)
            sums.append(jnp.dot(weights.astype(BF16), v2, preferred_element_type=F32))
        out[window, cols] = jnp.where(lane < 64, sums[0], sums[1]).astype(BF16)
    out[window, 512:640] = stats.astype(BF16)


def attend(info, gains, x_parts, w_parts):
    anywhere = pl.BlockSpec(memory_space=pl.ANY)
    inside = pl.BlockSpec(memory_space=pltpu.VMEM)
    return pl.pallas_call(
        attend_kernel,
        in_specs=[pl.BlockSpec(memory_space=pltpu.SMEM), inside] + [anywhere] * 18,
        out_specs=inside,
        out_shape=jax.ShapeDtypeStruct((512, 640), BF16),
        scratch_shapes=[
            pltpu.VMEM((640, 4096), BF16),
            pltpu.VMEM((32, 384, 512), BF16),
            pltpu.VMEM((512, 512), BF16),
            pltpu.VMEM((512, 512), BF16),
            pltpu.VMEM((128, 512), BF16),
            pltpu.VMEM((640, 128), F32),
            pltpu.SemaphoreType.DMA((2,)),
        ],
        compiler_params=pltpu.CompilerParams(vmem_limit_bytes=40 * 2**20),
        cost_estimate=pl.CostEstimate(
            flops=5 * 10**9, bytes_accessed=30 * 2**20, transcendentals=2**19
        ),
        name="project_attend",
    )(info, gains, *x_parts, *w_parts)


def merge_kernel(info, got, *refs):
    w_parts = refs[:10]
    out, wo, sem = refs[10:]
    for ref, row, s in shard_places(w_parts, info[0]):
        pltpu.make_async_copy(
            ref.at[pl.ds(row * 512 + 384, 128)],
            wo.at[pl.ds(pl.multiple_of(s * 128, 128), 128)],
            sem,
        ).start()
    st = got[:, 512:640].astype(F32)
    both = st + pltpu.roll(st, 120, 1)
    sum_a = pltpu.roll(both, 112, 1).reshape(32, 16, 128)
    sum_b = pltpu.roll(both, 96, 1).reshape(32, 16, 128)
    both = both.reshape(32, 16, 128)
    lane3 = lax.broadcasted_iota(jnp.int32, (32, 16, 128), 2)
    head = lane3 < 8
    tops = jnp.where(head, both, 0.0)
    top = jnp.max(tops, axis=0, keepdims=True)
    factor = jnp.exp(tops - top)
    sum_a = jnp.where(head, sum_a * factor, 0.0)
    sum_b = jnp.where(head, sum_b * factor, 0.0)
    total = jnp.sum(sum_a + sum_b, axis=0, keepdims=True)
    inverse = jnp.where(head[:1], 1.0 / total, 0.0)
    share_a = jnp.sum((sum_a * inverse).reshape(512, 128), axis=1, keepdims=True)
    share_b = jnp.sum((sum_b * inverse).reshape(512, 128), axis=1, keepdims=True)
    lane = lax.broadcasted_iota(jnp.int32, (512, 128), 1)
    slot = (lax.broadcasted_iota(jnp.int32, (512, 128), 0) // 16) * 2
    pooled = jnp.sum(
        jnp.where(lane == slot, share_a, 0.0) + jnp.where(lane == slot + 1, share_b, 0.0),
        axis=0,
        keepdims=True,
    )
    ratio_hi, ratio_lo = high_low((factor * inverse).reshape(512, 128))
    spread = (
        lax.broadcasted_iota(jnp.int32, (128, 512), 1) // HEAD_DIM
        == lax.broadcasted_iota(jnp.int32, (128, 512), 0)
    )
    spread = jnp.where(spread, 1.0, 0.0).astype(BF16)
    ratio = jnp.dot(ratio_hi.astype(BF16), spread, preferred_element_type=F32) + jnp.dot(
        ratio_lo.astype(BF16), spread, preferred_element_type=F32
    )
    context = jnp.sum((got[:, 0:512].astype(F32) * ratio).reshape(32, 16, 512), axis=0)
    context = context.astype(BF16)
    pool_hi, pool_lo = high_low(pooled)
    row = lax.broadcasted_iota(jnp.int32, (16, 128), 0)
    extra = jnp.where(row == 0, pool_hi, jnp.where(row == 1, pool_lo, 0.0)).astype(BF16)
    pltpu.make_async_copy(wo, wo, sem).wait()
    for z in range(8):
        term = lax.dot_general(
            context,
            wo[512 * z : 512 * (z + 1), :],
            (((1,), (1,)), ((), ())),
            preferred_element_type=F32,
        )
        out[z, :, 0:512] = term.astype(BF16)
        out[z, :, 512:640] = extra


def merge(info, got, w_parts):
    anywhere = pl.BlockSpec(memory_space=pl.ANY)
    inside = pl.BlockSpec(memory_space=pltpu.VMEM)
    return pl.pallas_call(
        merge_kernel,
        in_specs=[pl.BlockSpec(memory_space=pltpu.SMEM), inside] + [anywhere] * 10,
        out_specs=inside,
        out_shape=jax.ShapeDtypeStruct((8, 16, 640), BF16),
        scratch_shapes=[pltpu.VMEM((4096, 512), BF16), pltpu.SemaphoreType.DMA(())],
        compiler_params=pltpu.CompilerParams(vmem_limit_bytes=40 * 2**20),
        name="merge_project",
    )(info, got, *w_parts)


def add_kernel(got, rows, out):
    sums = jnp.sum(got[...].astype(F32), axis=0)
    done = (rows[...].astype(F32) + sums[:, 0:512]).astype(BF16)
    pool_hi, pool_lo = high_low(jnp.sum(sums[:, 512:640], axis=0, keepdims=True))
    row = lax.broadcasted_iota(jnp.int32, (16, 128), 0)
    extra = jnp.where(row == 0, pool_hi, jnp.where(row == 1, pool_lo, 0.0)).astype(BF16)
    for s in range(32):
        out[s, :, 0:512] = done
        out[s, :, 512:640] = extra


def add_rows(got, rows):
    return pl.pallas_call(
        add_kernel,
        out_shape=jax.ShapeDtypeStruct((32, 16, 640), BF16),
        name="add_rows",
    )(got, rows)


def on_device(
    encoded, decoder_states, passage_counts, enc_gain, dec_gain, w_key, w_value, w_query, w_out
):
    sec = lax.axis_index("sec")
    tp = lax.axis_index("tp")
    questions = decoder_states.shape[0] // QTOK
    ends = jnp.cumsum(passage_counts)
    slots = sec * 2 + jnp.arange(2, dtype=jnp.int32)
    owner = jnp.sum((slots[:, None] >= ends[None, :]).astype(jnp.int32), axis=1)
    first = jnp.minimum(owner[0], questions - 2)
    info = jnp.stack([sec, tp, first, owner[0], owner[1]]).astype(jnp.int32)
    window = lax.dynamic_slice_in_dim(decoder_states, first * QTOK, 2 * QTOK, 0)
    x_parts = ring_gather(jnp.concatenate([encoded, window], 0))
    w_parts = plane_gather(jnp.concatenate([w_key, w_value, w_query, w_out.T], 0))
    gains = jnp.stack([enc_gain, dec_gain])
    partial = attend(info, gains, x_parts, w_parts)
    got = lax.all_to_all(partial, "sec", 0, 0, tiled=True)
    terms = merge(info, got, w_parts)
    terms = lax.all_to_all(terms, "tp", 0, 0, tiled=True)
    rows = lax.dynamic_slice_in_dim(decoder_states, sec * 16, 16, 0)
    finished = lax.all_to_all(add_rows(terms, rows), "sec", 0, 0, tiled=True)
    decoded = finished[:, :, 0:512].reshape(512, 512)
    pooled = jnp.sum(finished[:, 0:2, 512:640].astype(F32), axis=(0, 1))
    passage_scores = lax.dynamic_slice_in_dim(pooled, sec * 2, 2, 0) / (HEADS * QTOK)
    return (decoded, passage_scores)


def solution(mesh):
    placed = (
        P("sec", "tp"),
        P(None, "tp"),
        P(),
        P(),
        P(),
        P("sec", "tp"),
        P("sec", "tp"),
        P("sec", "tp"),
        P("tp", "sec"),
    )
    return jax.shard_map(
        on_device, mesh=mesh, in_specs=placed, out_specs=(P(None, "tp"), P("sec")), check_vma=False
    )
```

```python
import jax
import jax.numpy as jnp
from jax import lax
from jax.experimental import pallas as pl
from jax.experimental.pallas import tpu as pltpu
from jax.sharding import PartitionSpec as P

HEADS = 64
HEAD_DIM = 64
PTOK = 256
QTOK = 64
SIDE = 4
CORES = 2
ABSENT = -1e30
BF16 = jnp.bfloat16
F32 = jnp.float32
REACH = (0, -1, 1, 2)


def sec_id(x, y, c):
    return ((x % SIDE) * SIDE + y % SIDE) * CORES + c


def along_tp(v, step):
    n = lax.axis_size("tp")
    return lax.ppermute(v, "tp", [(i, (i + step) % n) for i in range(n)])


def along_tp_by_core(v):
    n = lax.axis_size("tp")
    s = lax.axis_size("sec")
    pairs = [
        (i * n + z, i * n + (z + (1 if i % CORES == 0 else -1)) % n)
        for i in range(s)
        for z in range(n)
    ]
    return lax.ppermute(v, ("sec", "tp"), pairs)


def other_core(v):
    s = lax.axis_size("sec")
    return lax.ppermute(v, "sec", [(i, i ^ 1) for i in range(s)])


def in_plane(v, step, swap):
    pairs = []
    for x in range(SIDE):
        for y in range(SIDE):
            for c in range(CORES):
                on_x = (c == 0) != swap
                to = sec_id(x + step, y, c) if on_x else sec_id(x, y + step, c)
                pairs.append((sec_id(x, y, c), to))
    return lax.ppermute(v, "sec", pairs)


def gather(tokens, shard):
    together = lax.optimization_barrier
    half = shard.shape[0] // 2
    theirs = other_core(tokens)
    mine1, theirs1 = along_tp_by_core(tokens), along_tp_by_core(theirs)
    a, b = in_plane(shard, 1, False), in_plane(shard, -1, False)
    a, b, mine1 = together((a, b, mine1))
    c, d = in_plane(a[:half], 1, False), in_plane(b[half:], -1, False)
    mine2 = along_tp_by_core(mine1)
    c, d, theirs1 = together((c, d, theirs1))
    theirs2 = along_tp_by_core(theirs1)
    g = jnp.concatenate([shard, a, b, c, d], 0)
    g2, mine2 = together((g, mine2))
    ga, gb = in_plane(g, 1, True), in_plane(g2, -1, True)
    mine3 = along_tp_by_core(mine2)
    passed1 = other_core(theirs1)
    theirs3 = along_tp_by_core(theirs2)
    mine4 = along_tp_by_core(mine3)
    passed2, go = other_core(theirs2), other_core(g2)
    ga, mine3, passed1 = together((ga, mine3, passed1))
    half = g.shape[0] // 2
    gc, gd = in_plane(ga[:half], 1, True), in_plane(gb[half:], -1, True)
    theirs3, ga2, gb2, mine4, passed2 = together((theirs3, ga, gb, mine4, passed2))
    passed3, gao, gbo = other_core(theirs3), other_core(ga2), other_core(gb2)
    gc, gd, mine4 = together((gc, gd, mine4))
    held = [tokens, mine1, mine2, mine3, mine4, passed1, passed2, passed3]
    return held, [g, ga, gb, gc, gd, go, gao, gbo, other_core(gc), other_core(gd)]


def high_low(v):
    high = v.astype(BF16).astype(F32)
    return high, (v - high).astype(BF16).astype(F32)


def shard_places(w_parts, sec):
    core = sec % CORES
    px = sec // (SIDE * CORES)
    py = (sec // CORES) % SIDE
    shards = []
    for mine in (True, False):
        group = w_parts[:5] if mine else w_parts[5:]
        col = core if mine else 1 - core
        for r2 in REACH:
            for at, r1 in enumerate(REACH):
                if r2 == 2:
                    ref, row = (group[3], at) if at < 2 else (group[4], at - 2)
                else:
                    ref, row = group[REACH.index(r2)], at
                dx = jnp.where(col == 0, r1, r2)
                dy = jnp.where(col == 0, r2, r1)
                s = (((px + dx + SIDE) % SIDE) * SIDE + (py + dy + SIDE) % SIDE) * CORES + col
                shards.append((ref, row, s))
    return shards


def attend_kernel(info, gains, *refs):
    x_parts, w_parts = refs[:8], refs[8:18]
    out, xs, ws, ks, vs, qs, scale, sems = refs[18:]
    sec, tp, first, own_a, own_b = (info[i] for i in range(5))
    turn = 2 * (sec % CORES) - 1
    for part, off in zip(x_parts, (0, 1, 2, 3, 4, -1, -2, -3)):
        at = pl.multiple_of(((tp + turn * off + 8) % 8) * 512, 512)
        pltpu.make_async_copy(part, xs.at[:, pl.ds(at, 512)], sems.at[0]).start()
    shards = shard_places(w_parts, sec)
    for kind in (2, 0, 1):
        for ref, row, s in shards:
            pltpu.make_async_copy(
                ref.at[pl.ds(row * 512 + kind * 128, 128)], ws.at[kind, s], sems.at[1 + kind]
            ).start()
    lane = lax.broadcasted_iota(jnp.int32, (1, 128), 1)
    rest = jnp.where(lane < 8, ABSENT, 0.0)
    out[:, :512] = jnp.zeros((512, 512), BF16)
    out[:, 512:] = jnp.broadcast_to(rest, (512, 128)).astype(BF16)

    pltpu.make_async_copy(xs, xs, sems.at[0]).wait()

    @pl.loop(0, 5)
    def _(i):
        rows = pl.ds(pl.multiple_of(i * 128, 128), 128)
        which = pl.ds((i == 4).astype(jnp.int32), 1)
        total = jnp.zeros((128, 1), F32)
        for j in range(8):
            cols = slice(512 * j, 512 * (j + 1))
            v = xs[rows, cols].astype(F32)
            total = total + jnp.sum(v * v, axis=1, keepdims=True)
            xs[rows, cols] = (v * gains[which, cols]).astype(BF16)
        scale[rows, :] = jnp.broadcast_to(lax.rsqrt(total / 4096.0 + 1e-06), (128, 128))

    for kind, rows, held in ((2, slice(512, 640), qs), (0, slice(0, 512), ks), (1, slice(0, 512), vs)):
        pltpu.make_async_copy(ws.at[kind], ws.at[kind], sems.at[1 + kind]).wait()

        @pl.loop(0, 2)
        def _(n):
            cols = pl.ds(pl.multiple_of(n * 256, 256), 256)
            part = ws[kind, :, :, cols].reshape(4096, 256)
            product = jnp.dot(xs[rows, :], part, preferred_element_type=F32)
            held[:, cols] = (product * scale[rows, 0:1]).astype(BF16)

    row_owner = first + lax.broadcasted_iota(jnp.int32, (128, 512), 0) // QTOK
    key_owner = jnp.where(lax.broadcasted_iota(jnp.int32, (128, 512), 1) < PTOK, own_a, own_b)
    keep = row_owner == key_owner
    window = pl.ds(pl.multiple_of(first * QTOK, QTOK), 128)
    lane = lax.broadcasted_iota(jnp.int32, (128, 128), 1)
    stats = jnp.zeros((128, 128), F32)
    for pair in range(4):
        cols = slice(128 * pair, 128 * (pair + 1))
        q2, k2, v2 = qs[:, cols], ks[:, cols], vs[:, cols]
        sums = []
        for side in range(2):
            h = 2 * pair + side
            mine = (lane < 64) if side == 0 else (lane >= 64)
            qh = jnp.where(mine, q2.astype(F32), 0.0).astype(BF16)
            scores = lax.dot_general(qh, k2, (((1,), (1,)), ((), ())), preferred_element_type=F32)
            scores = jnp.where(keep, scores, ABSENT)
            top_hi, top_lo = high_low(jnp.max(scores, axis=1, keepdims=True))
            weights = jnp.where(keep, jnp.exp(scores - (top_hi + top_lo)), 0.0)
            a_hi, a_lo = high_low(jnp.sum(weights[:, :PTOK], axis=1, keepdims=True))
            b_hi, b_lo = high_low(jnp.sum(weights[:, PTOK:], axis=1, keepdims=True))
            for at, value in enumerate((top_hi, top_lo, a_hi, a_lo, b_hi, b_lo)):
                stats = jnp.where(lane == 8 * at + h, value, stats)
            sums.append(jnp.dot(weights.astype(BF16), v2, preferred_element_type=F32))
        out[window, cols] = jnp.where(lane < 64, sums[0], sums[1]).astype(BF16)
    out[window, 512:640] = stats.astype(BF16)


def attend(info, gains, x_parts, w_parts):
    anywhere = pl.BlockSpec(memory_space=pl.ANY)
    inside = pl.BlockSpec(memory_space=pltpu.VMEM)
    return pl.pallas_call(
        attend_kernel,
        in_specs=[pl.BlockSpec(memory_space=pltpu.SMEM), inside] + [anywhere] * 18,
        out_specs=inside,
        out_shape=jax.ShapeDtypeStruct((512, 640), BF16),
        scratch_shapes=[
            pltpu.VMEM((640, 4096), BF16),
            pltpu.VMEM((3, 32, 128, 512), BF16),
            pltpu.VMEM((512, 512), BF16),
            pltpu.VMEM((512, 512), BF16),
            pltpu.VMEM((128, 512), BF16),
            pltpu.VMEM((640, 128), F32),
            pltpu.SemaphoreType.DMA((4,)),
        ],
        compiler_params=pltpu.CompilerParams(vmem_limit_bytes=54 * 2**20),
        cost_estimate=pl.CostEstimate(
            flops=5 * 10**9, bytes_accessed=30 * 2**20, transcendentals=2**19
        ),
        name="project_attend",
    )(info, gains, *x_parts, *w_parts)


def assemble_kernel(info, *refs):
    w_parts = refs[:10]
    wo, sem = refs[10:]
    for ref, row, s in shard_places(w_parts, info[0]):
        pltpu.make_async_copy(
            ref.at[pl.ds(row * 512 + 384, 128)],
            wo.at[pl.ds(pl.multiple_of(s * 128, 128), 128)],
            sem,
        ).start()
    pltpu.make_async_copy(wo, wo, sem).wait()


def assemble(info, w_parts):
    anywhere = pl.BlockSpec(memory_space=pl.ANY)
    return pl.pallas_call(
        assemble_kernel,
        in_specs=[pl.BlockSpec(memory_space=pltpu.SMEM)] + [anywhere] * 10,
        out_specs=pl.BlockSpec(memory_space=pltpu.VMEM),
        out_shape=jax.ShapeDtypeStruct((4096, 512), BF16),
        scratch_shapes=[pltpu.SemaphoreType.DMA(())],
        compiler_params=pltpu.CompilerParams(vmem_limit_bytes=58 * 2**20),
        cost_estimate=pl.CostEstimate(flops=0, bytes_accessed=8 * 2**20, transcendentals=0),
        name="assemble_out",
    )(info, *w_parts)


def merge_kernel(got, wo, out):
    st = got[:, 512:640].astype(F32)
    both = st + pltpu.roll(st, 120, 1)
    sum_a = pltpu.roll(both, 112, 1).reshape(32, 16, 128)
    sum_b = pltpu.roll(both, 96, 1).reshape(32, 16, 128)
    both = both.reshape(32, 16, 128)
    lane3 = lax.broadcasted_iota(jnp.int32, (32, 16, 128), 2)
    head = lane3 < 8
    tops = jnp.where(head, both, 0.0)
    top = jnp.max(tops, axis=0, keepdims=True)
    factor = jnp.exp(tops - top)
    sum_a = jnp.where(head, sum_a * factor, 0.0)
    sum_b = jnp.where(head, sum_b * factor, 0.0)
    total = jnp.sum(sum_a + sum_b, axis=0, keepdims=True)
    inverse = jnp.where(head[:1], 1.0 / total, 0.0)
    share_a = jnp.sum((sum_a * inverse).reshape(512, 128), axis=1, keepdims=True)
    share_b = jnp.sum((sum_b * inverse).reshape(512, 128), axis=1, keepdims=True)
    lane = lax.broadcasted_iota(jnp.int32, (512, 128), 1)
    slot = (lax.broadcasted_iota(jnp.int32, (512, 128), 0) // 16) * 2
    pooled = jnp.sum(
        jnp.where(lane == slot, share_a, 0.0) + jnp.where(lane == slot + 1, share_b, 0.0),
        axis=0,
        keepdims=True,
    )
    ratio_hi, ratio_lo = high_low((factor * inverse).reshape(512, 128))
    spread = (
        lax.broadcasted_iota(jnp.int32, (128, 512), 1) // HEAD_DIM
        == lax.broadcasted_iota(jnp.int32, (128, 512), 0)
    )
    spread = jnp.where(spread, 1.0, 0.0).astype(BF16)
    ratio = jnp.dot(ratio_hi.astype(BF16), spread, preferred_element_type=F32) + jnp.dot(
        ratio_lo.astype(BF16), spread, preferred_element_type=F32
    )
    context = jnp.sum((got[:, 0:512].astype(F32) * ratio).reshape(32, 16, 512), axis=0)
    context = context.astype(BF16)
    pool_hi, pool_lo = high_low(pooled)
    row = lax.broadcasted_iota(jnp.int32, (16, 128), 0)
    extra = jnp.where(row == 0, pool_hi, jnp.where(row == 1, pool_lo, 0.0)).astype(BF16)
    for z in range(8):
        term = lax.dot_general(
            context,
            wo[512 * z : 512 * (z + 1), :],
            (((1,), (1,)), ((), ())),
            preferred_element_type=F32,
        )
        out[z, :, 0:512] = term.astype(BF16)
        out[z, :, 512:640] = extra


def merge(got, wo):
    return pl.pallas_call(
        merge_kernel,
        out_shape=jax.ShapeDtypeStruct((8, 16, 640), BF16),
        compiler_params=pltpu.CompilerParams(vmem_limit_bytes=58 * 2**20),
        name="merge_project",
    )(got, wo)


def add_kernel(got, rows, out):
    sums = jnp.sum(got[...].astype(F32), axis=0)
    done = (rows[...].astype(F32) + sums[:, 0:512]).astype(BF16)
    pool_hi, pool_lo = high_low(jnp.sum(sums[:, 512:640], axis=0, keepdims=True))
    row = lax.broadcasted_iota(jnp.int32, (16, 128), 0)
    extra = jnp.where(row == 0, pool_hi, jnp.where(row == 1, pool_lo, 0.0)).astype(BF16)
    for s in range(32):
        out[s, :, 0:512] = done
        out[s, :, 512:640] = extra


def add_rows(got, rows):
    return pl.pallas_call(
        add_kernel,
        out_shape=jax.ShapeDtypeStruct((32, 16, 640), BF16),
        name="add_rows",
    )(got, rows)


def pack_kernel(
    info, encoded, states, w_key, w_value, w_query, w_out, gain_a, gain_b, tokens, shard, gains
):
    gains[0:1, :] = gain_a[...]
    gains[1:2, :] = gain_b[...]
    tokens[0:512, :] = encoded[...]
    tokens[512:640, :] = states[pl.ds(pl.multiple_of(info[2] * QTOK, QTOK), 2 * QTOK), :]
    shard[0:128, :] = w_key[...]
    shard[128:256, :] = w_value[...]
    shard[256:384, :] = w_query[...]
    shard[384:512, :] = w_out[...].T


def pack(info, *arrays):
    inside = pl.BlockSpec(memory_space=pltpu.VMEM)
    return pl.pallas_call(
        pack_kernel,
        in_specs=[pl.BlockSpec(memory_space=pltpu.SMEM)] + [inside] * 8,
        out_specs=[inside] * 3,
        out_shape=[
            jax.ShapeDtypeStruct((640, 512), BF16),
            jax.ShapeDtypeStruct((512, 512), BF16),
            jax.ShapeDtypeStruct((2, 4096), F32),
        ],
        name="pack",
    )(info, *arrays)


def on_device(
    encoded, decoder_states, passage_counts, enc_gain, dec_gain, w_key, w_value, w_query, w_out
):
    sec = lax.axis_index("sec")
    tp = lax.axis_index("tp")
    questions = decoder_states.shape[0] // QTOK
    order = jnp.arange(questions, dtype=jnp.int32)
    ends = jnp.sum(jnp.where(order[:, None] <= order[None, :], passage_counts[:, None], 0), axis=0)
    slots = sec * 2 + jnp.arange(2, dtype=jnp.int32)
    owner = jnp.sum((slots[:, None] >= ends[None, :]).astype(jnp.int32), axis=1)
    first = jnp.minimum(owner[0], questions - 2)
    info = jnp.stack([sec, tp, first, owner[0], owner[1]]).astype(jnp.int32)
    tokens, shard, gains = pack(
        info,
        encoded,
        decoder_states,
        w_key,
        w_value,
        w_query,
        w_out,
        enc_gain.reshape(1, -1),
        dec_gain.reshape(1, -1),
    )
    x_parts, w_parts = gather(tokens, shard)
    partial = attend(info, gains, x_parts, w_parts)
    got = lax.all_to_all(partial, "sec", 0, 0, tiled=True)
    terms = merge(got, assemble(info, w_parts))
    terms = lax.all_to_all(terms, "tp", 0, 0, tiled=True)
    rows = lax.dynamic_slice_in_dim(decoder_states, sec * 16, 16, 0)
    finished = lax.all_to_all(add_rows(terms, rows), "sec", 0, 0, tiled=True)
    decoded = finished[:, :, 0:512].reshape(512, 512)
    pooled = jnp.sum(finished[:, 0:2, 512:640].astype(F32), axis=(0, 1))
    passage_scores = lax.dynamic_slice_in_dim(pooled, sec * 2, 2, 0) / (HEADS * QTOK)
    return (decoded, passage_scores)


def solution(mesh):
    placed = (
        P("sec", "tp"),
        P(None, "tp"),
        P(),
        P(),
        P(),
        P("sec", "tp"),
        P("sec", "tp"),
        P("sec", "tp"),
        P("tp", "sec"),
    )
    return jax.shard_map(
        on_device, mesh=mesh, in_specs=placed, out_specs=(P(None, "tp"), P("sec")), check_vma=False
    )
```

```python
import jax
import jax.numpy as jnp
from jax import lax
from jax.experimental import pallas as pl
from jax.experimental.pallas import tpu as pltpu
from jax.sharding import PartitionSpec as P

HEADS = 64
HEAD_DIM = 64
PTOK = 256
QTOK = 64
SIDE = 4
CORES = 2
ABSENT = -1e30
BF16 = jnp.bfloat16
F32 = jnp.float32
REACH = (0, -1, 1, 2)


def sec_id(x, y, c):
    return ((x % SIDE) * SIDE + y % SIDE) * CORES + c


def along_tp(v, step):
    n = lax.axis_size("tp")
    return lax.ppermute(v, "tp", [(i, (i + step) % n) for i in range(n)])


def along_tp_by_core(v):
    n = lax.axis_size("tp")
    s = lax.axis_size("sec")
    pairs = [
        (i * n + z, i * n + (z + (1 if i % CORES == 0 else -1)) % n)
        for i in range(s)
        for z in range(n)
    ]
    return lax.ppermute(v, ("sec", "tp"), pairs)


def other_core(v):
    s = lax.axis_size("sec")
    return lax.ppermute(v, "sec", [(i, i ^ 1) for i in range(s)])


def in_plane(v, step, swap):
    pairs = []
    for x in range(SIDE):
        for y in range(SIDE):
            for c in range(CORES):
                on_x = (c == 0) != swap
                to = sec_id(x + step, y, c) if on_x else sec_id(x, y + step, c)
                pairs.append((sec_id(x, y, c), to))
    return lax.ppermute(v, "sec", pairs)


def ring_gather(piece):
    core = lax.axis_index("sec") % CORES
    up = down = piece
    held = [piece]
    for _ in range(3):
        up, down = along_tp(up, 1), along_tp(down, -1)
        held += [up, down]
    held.append(along_tp_by_core(jnp.where(core == 0, up, down)))
    return held


def plane_gather(shard):
    half = shard.shape[0] // 2
    a, b = in_plane(shard, 1, False), in_plane(shard, -1, False)
    c, d = in_plane(a[:half], 1, False), in_plane(b[half:], -1, False)
    g = jnp.concatenate([shard, a, b, c, d], 0)
    ga, gb = in_plane(g, 1, True), in_plane(g, -1, True)
    half = g.shape[0] // 2
    gc, gd = in_plane(ga[:half], 1, True), in_plane(gb[half:], -1, True)
    own = [g, ga, gb, gc, gd]
    return own + [other_core(v) for v in own]


def high_low(v):
    high = v.astype(BF16).astype(F32)
    return high, (v - high).astype(BF16).astype(F32)


def shard_places(w_parts, sec):
    core = sec % CORES
    px = sec // (SIDE * CORES)
    py = (sec // CORES) % SIDE
    shards = []
    for mine in (True, False):
        group = w_parts[:5] if mine else w_parts[5:]
        col = core if mine else 1 - core
        for r2 in REACH:
            for at, r1 in enumerate(REACH):
                if r2 == 2:
                    ref, row = (group[3], at) if at < 2 else (group[4], at - 2)
                else:
                    ref, row = group[REACH.index(r2)], at
                dx = jnp.where(col == 0, r1, r2)
                dy = jnp.where(col == 0, r2, r1)
                s = (((px + dx + SIDE) % SIDE) * SIDE + (py + dy + SIDE) % SIDE) * CORES + col
                shards.append((ref, row, s))
    return shards


def attend_kernel(info, gains, *refs):
    x_parts, w_parts = refs[:8], refs[8:18]
    out, xs, ws, ks, vs, qs, scale, sems = refs[18:]
    sec, tp, first, own_a, own_b = (info[i] for i in range(5))
    for part, off in zip(x_parts, (0, -1, 1, -2, 2, -3, 3, 4)):
        at = pl.multiple_of(((tp + off + 8) % 8) * 512, 512)
        pltpu.make_async_copy(part, xs.at[:, pl.ds(at, 512)], sems.at[0]).start()
    shards = shard_places(w_parts, sec)
    for ref, row, s in shards:
        pltpu.make_async_copy(ref.at[pl.ds(row * 512, 384)], ws.at[s], sems.at[1]).start()
    lane = lax.broadcasted_iota(jnp.int32, (1, 128), 1)
    rest = jnp.where(lane < 8, ABSENT, 0.0)
    out[:, :512] = jnp.zeros((512, 512), BF16)
    out[:, 512:] = jnp.broadcast_to(rest, (512, 128)).astype(BF16)

    pltpu.make_async_copy(xs, xs, sems.at[0]).wait()

    @pl.loop(0, 5)
    def _(i):
        rows = pl.ds(pl.multiple_of(i * 128, 128), 128)
        which = pl.ds((i == 4).astype(jnp.int32), 1)
        total = jnp.zeros((128, 1), F32)
        for j in range(8):
            cols = slice(512 * j, 512 * (j + 1))
            v = xs[rows, cols].astype(F32)
            total = total + jnp.sum(v * v, axis=1, keepdims=True)
            xs[rows, cols] = (v * gains[which, cols]).astype(BF16)
        scale[rows, :] = jnp.broadcast_to(lax.rsqrt(total / 4096.0 + 1e-06), (128, 128))

    pltpu.make_async_copy(ws, ws, sems.at[1]).wait()

    @pl.loop(0, 2)
    def _(n):
        cols = pl.ds(pl.multiple_of(n * 256, 256), 256)
        wq = ws[:, 256:384, cols].reshape(4096, 256)
        q = jnp.dot(xs[512:640, :], wq, preferred_element_type=F32)
        qs[:, cols] = (q * scale[512:640, 0:1]).astype(BF16)
        wk = ws[:, 0:128, cols].reshape(4096, 256)
        k = jnp.dot(xs[0:512, :], wk, preferred_element_type=F32)
        ks[:, cols] = (k * scale[0:512, 0:1]).astype(BF16)
        wv = ws[:, 128:256, cols].reshape(4096, 256)
        v = jnp.dot(xs[0:512, :], wv, preferred_element_type=F32)
        vs[:, cols] = (v * scale[0:512, 0:1]).astype(BF16)

    row_owner = first + lax.broadcasted_iota(jnp.int32, (128, 512), 0) // QTOK
    key_owner = jnp.where(lax.broadcasted_iota(jnp.int32, (128, 512), 1) < PTOK, own_a, own_b)
    keep = row_owner == key_owner
    window = pl.ds(pl.multiple_of(first * QTOK, QTOK), 128)
    lane = lax.broadcasted_iota(jnp.int32, (128, 128), 1)
    stats = jnp.zeros((128, 128), F32)
    for pair in range(4):
        cols = slice(128 * pair, 128 * (pair + 1))
        q2, k2, v2 = qs[:, cols], ks[:, cols], vs[:, cols]
        sums = []
        for side in range(2):
            h = 2 * pair + side
            mine = (lane < 64) if side == 0 else (lane >= 64)
            qh = jnp.where(mine, q2.astype(F32), 0.0).astype(BF16)
            scores = lax.dot_general(qh, k2, (((1,), (1,)), ((), ())), preferred_element_type=F32)
            scores = jnp.where(keep, scores, ABSENT)
            top_hi, top_lo = high_low(jnp.max(scores, axis=1, keepdims=True))
            weights = jnp.where(keep, jnp.exp(scores - (top_hi + top_lo)), 0.0)
            a_hi, a_lo = high_low(jnp.sum(weights[:, :PTOK], axis=1, keepdims=True))
            b_hi, b_lo = high_low(jnp.sum(weights[:, PTOK:], axis=1, keepdims=True))
            for at, value in enumerate((top_hi, top_lo, a_hi, a_lo, b_hi, b_lo)):
                stats = jnp.where(lane == 8 * at + h, value, stats)
            sums.append(jnp.dot(weights.astype(BF16), v2, preferred_element_type=F32))
        out[window, cols] = jnp.where(lane < 64, sums[0], sums[1]).astype(BF16)
    out[window, 512:640] = stats.astype(BF16)


def attend(info, gains, x_parts, w_parts):
    anywhere = pl.BlockSpec(memory_space=pl.ANY)
    inside = pl.BlockSpec(memory_space=pltpu.VMEM)
    return pl.pallas_call(
        attend_kernel,
        in_specs=[pl.BlockSpec(memory_space=pltpu.SMEM), inside] + [anywhere] * 18,
        out_specs=inside,
        out_shape=jax.ShapeDtypeStruct((512, 640), BF16),
        scratch_shapes=[
            pltpu.VMEM((640, 4096), BF16),
            pltpu.VMEM((32, 384, 512), BF16),
            pltpu.VMEM((512, 512), BF16),
            pltpu.VMEM((512, 512), BF16),
            pltpu.VMEM((128, 512), BF16),
            pltpu.VMEM((640, 128), F32),
            pltpu.SemaphoreType.DMA((2,)),
        ],
        compiler_params=pltpu.CompilerParams(vmem_limit_bytes=40 * 2**20),
        cost_estimate=pl.CostEstimate(
            flops=5 * 10**9, bytes_accessed=30 * 2**20, transcendentals=2**19
        ),
        name="project_attend",
    )(info, gains, *x_parts, *w_parts)


def assemble_kernel(info, *refs):
    w_parts = refs[:10]
    wo, sem = refs[10:]
    for ref, row, s in shard_places(w_parts, info[0]):
        pltpu.make_async_copy(
            ref.at[pl.ds(row * 512 + 384, 128)],
            wo.at[pl.ds(pl.multiple_of(s * 128, 128), 128)],
            sem,
        ).start()
    pltpu.make_async_copy(wo, wo, sem).wait()


def assemble(info, w_parts):
    anywhere = pl.BlockSpec(memory_space=pl.ANY)
    return pl.pallas_call(
        assemble_kernel,
        in_specs=[pl.BlockSpec(memory_space=pltpu.SMEM)] + [anywhere] * 10,
        out_specs=pl.BlockSpec(memory_space=pltpu.VMEM),
        out_shape=jax.ShapeDtypeStruct((4096, 512), BF16),
        scratch_shapes=[pltpu.SemaphoreType.DMA(())],
        compiler_params=pltpu.CompilerParams(vmem_limit_bytes=40 * 2**20),
        cost_estimate=pl.CostEstimate(flops=0, bytes_accessed=8 * 2**20, transcendentals=0),
        name="assemble_out",
    )(info, *w_parts)


def merge_kernel(got, wo, out):
    st = got[:, 512:640].astype(F32)
    both = st + pltpu.roll(st, 120, 1)
    sum_a = pltpu.roll(both, 112, 1).reshape(32, 16, 128)
    sum_b = pltpu.roll(both, 96, 1).reshape(32, 16, 128)
    both = both.reshape(32, 16, 128)
    lane3 = lax.broadcasted_iota(jnp.int32, (32, 16, 128), 2)
    head = lane3 < 8
    tops = jnp.where(head, both, 0.0)
    top = jnp.max(tops, axis=0, keepdims=True)
    factor = jnp.exp(tops - top)
    sum_a = jnp.where(head, sum_a * factor, 0.0)
    sum_b = jnp.where(head, sum_b * factor, 0.0)
    total = jnp.sum(sum_a + sum_b, axis=0, keepdims=True)
    inverse = jnp.where(head[:1], 1.0 / total, 0.0)
    share_a = jnp.sum((sum_a * inverse).reshape(512, 128), axis=1, keepdims=True)
    share_b = jnp.sum((sum_b * inverse).reshape(512, 128), axis=1, keepdims=True)
    lane = lax.broadcasted_iota(jnp.int32, (512, 128), 1)
    slot = (lax.broadcasted_iota(jnp.int32, (512, 128), 0) // 16) * 2
    pooled = jnp.sum(
        jnp.where(lane == slot, share_a, 0.0) + jnp.where(lane == slot + 1, share_b, 0.0),
        axis=0,
        keepdims=True,
    )
    ratio_hi, ratio_lo = high_low((factor * inverse).reshape(512, 128))
    spread = (
        lax.broadcasted_iota(jnp.int32, (128, 512), 1) // HEAD_DIM
        == lax.broadcasted_iota(jnp.int32, (128, 512), 0)
    )
    spread = jnp.where(spread, 1.0, 0.0).astype(BF16)
    ratio = jnp.dot(ratio_hi.astype(BF16), spread, preferred_element_type=F32) + jnp.dot(
        ratio_lo.astype(BF16), spread, preferred_element_type=F32
    )
    context = jnp.sum((got[:, 0:512].astype(F32) * ratio).reshape(32, 16, 512), axis=0)
    context = context.astype(BF16)
    pool_hi, pool_lo = high_low(pooled)
    row = lax.broadcasted_iota(jnp.int32, (16, 128), 0)
    extra = jnp.where(row == 0, pool_hi, jnp.where(row == 1, pool_lo, 0.0)).astype(BF16)
    for z in range(8):
        term = lax.dot_general(
            context,
            wo[512 * z : 512 * (z + 1), :],
            (((1,), (1,)), ((), ())),
            preferred_element_type=F32,
        )
        out[z, :, 0:512] = term.astype(BF16)
        out[z, :, 512:640] = extra


def merge(got, wo):
    return pl.pallas_call(
        merge_kernel,
        out_shape=jax.ShapeDtypeStruct((8, 16, 640), BF16),
        compiler_params=pltpu.CompilerParams(vmem_limit_bytes=40 * 2**20),
        name="merge_project",
    )(got, wo)


def add_kernel(got, rows, out):
    sums = jnp.sum(got[...].astype(F32), axis=0)
    done = (rows[...].astype(F32) + sums[:, 0:512]).astype(BF16)
    pool_hi, pool_lo = high_low(jnp.sum(sums[:, 512:640], axis=0, keepdims=True))
    row = lax.broadcasted_iota(jnp.int32, (16, 128), 0)
    extra = jnp.where(row == 0, pool_hi, jnp.where(row == 1, pool_lo, 0.0)).astype(BF16)
    for s in range(32):
        out[s, :, 0:512] = done
        out[s, :, 512:640] = extra


def add_rows(got, rows):
    return pl.pallas_call(
        add_kernel,
        out_shape=jax.ShapeDtypeStruct((32, 16, 640), BF16),
        name="add_rows",
    )(got, rows)


def pack_kernel(
    info, encoded, states, w_key, w_value, w_query, w_out, tokens, shard
):
    tokens[0:512, :] = encoded[...]
    tokens[512:640, :] = states[pl.ds(pl.multiple_of(info[2] * QTOK, QTOK), 2 * QTOK), :]
    shard[0:128, :] = w_key[...]
    shard[128:256, :] = w_value[...]
    shard[256:384, :] = w_query[...]
    shard[384:512, :] = w_out[...].T


def pack(info, *arrays):
    inside = pl.BlockSpec(memory_space=pltpu.VMEM)
    return pl.pallas_call(
        pack_kernel,
        in_specs=[pl.BlockSpec(memory_space=pltpu.SMEM)] + [inside] * 6,
        out_specs=[inside] * 2,
        out_shape=[
            jax.ShapeDtypeStruct((640, 512), BF16),
            jax.ShapeDtypeStruct((512, 512), BF16),
        ],
        name="pack",
    )(info, *arrays)


def on_device(
    encoded, decoder_states, passage_counts, enc_gain, dec_gain, w_key, w_value, w_query, w_out
):
    sec = lax.axis_index("sec")
    tp = lax.axis_index("tp")
    questions = decoder_states.shape[0] // QTOK
    order = jnp.arange(questions, dtype=jnp.int32)
    ends = jnp.sum(jnp.where(order[:, None] <= order[None, :], passage_counts[:, None], 0), axis=0)
    slots = sec * 2 + jnp.arange(2, dtype=jnp.int32)
    owner = jnp.sum((slots[:, None] >= ends[None, :]).astype(jnp.int32), axis=1)
    first = jnp.minimum(owner[0], questions - 2)
    info = jnp.stack([sec, tp, first, owner[0], owner[1]]).astype(jnp.int32)
    tokens, shard = pack(info, encoded, decoder_states, w_key, w_value, w_query, w_out)
    x_parts = ring_gather(tokens)
    w_parts = plane_gather(shard)
    gains = jnp.stack([enc_gain, dec_gain])
    partial = attend(info, gains, x_parts, w_parts)
    got = lax.all_to_all(partial, "sec", 0, 0, tiled=True)
    terms = merge(got, assemble(info, w_parts))
    terms = lax.all_to_all(terms, "tp", 0, 0, tiled=True)
    rows = lax.dynamic_slice_in_dim(decoder_states, sec * 16, 16, 0)
    finished = lax.all_to_all(add_rows(terms, rows), "sec", 0, 0, tiled=True)
    decoded = finished[:, :, 0:512].reshape(512, 512)
    pooled = jnp.sum(finished[:, 0:2, 512:640].astype(F32), axis=(0, 1))
    passage_scores = lax.dynamic_slice_in_dim(pooled, sec * 2, 2, 0) / (HEADS * QTOK)
    return (decoded, passage_scores)


def solution(mesh):
    placed = (
        P("sec", "tp"),
        P(None, "tp"),
        P(),
        P(),
        P(),
        P("sec", "tp"),
        P("sec", "tp"),
        P("sec", "tp"),
        P("tp", "sec"),
    )
    return jax.shard_map(
        on_device, mesh=mesh, in_specs=placed, out_specs=(P(None, "tp"), P("sec")), check_vma=False
    )
```

```python
import jax
import jax.numpy as jnp
from jax import lax
from jax.experimental import pallas as pl
from jax.experimental.pallas import tpu as pltpu
from jax.sharding import PartitionSpec as P

HEADS = 64
HEAD_DIM = 64
PTOK = 256
QTOK = 64
SIDE = 4
CORES = 2
ABSENT = -1e30
BF16 = jnp.bfloat16
F32 = jnp.float32
REACH = (0, -1, 1, 2)


def sec_id(x, y, c):
    return ((x % SIDE) * SIDE + y % SIDE) * CORES + c


def along_tp(v, step):
    n = lax.axis_size("tp")
    return lax.ppermute(v, "tp", [(i, (i + step) % n) for i in range(n)])


def along_tp_by_core(v):
    n = lax.axis_size("tp")
    s = lax.axis_size("sec")
    pairs = [
        (i * n + z, i * n + (z + (1 if i % CORES == 0 else -1)) % n)
        for i in range(s)
        for z in range(n)
    ]
    return lax.ppermute(v, ("sec", "tp"), pairs)


def other_core(v):
    s = lax.axis_size("sec")
    return lax.ppermute(v, "sec", [(i, i ^ 1) for i in range(s)])


def in_plane(v, step, swap):
    pairs = []
    for x in range(SIDE):
        for y in range(SIDE):
            for c in range(CORES):
                on_x = (c == 0) != swap
                to = sec_id(x + step, y, c) if on_x else sec_id(x, y + step, c)
                pairs.append((sec_id(x, y, c), to))
    return lax.ppermute(v, "sec", pairs)


def gather(tokens, shard):
    together = lax.optimization_barrier
    half = shard.shape[0] // 2
    theirs = other_core(tokens)
    mine1, theirs1 = along_tp_by_core(tokens), along_tp_by_core(theirs)
    a, b = in_plane(shard, 1, False), in_plane(shard, -1, False)
    a, b, mine1 = together((a, b, mine1))
    c, d = in_plane(a[:half], 1, False), in_plane(b[half:], -1, False)
    mine2 = along_tp_by_core(mine1)
    c, d, theirs1 = together((c, d, theirs1))
    theirs2 = along_tp_by_core(theirs1)
    g = jnp.concatenate([shard, a, b, c, d], 0)
    g2, mine2 = together((g, mine2))
    ga, gb = in_plane(g, 1, True), in_plane(g2, -1, True)
    mine3 = along_tp_by_core(mine2)
    passed1 = other_core(theirs1)
    theirs3 = along_tp_by_core(theirs2)
    mine4 = along_tp_by_core(mine3)
    passed2, go = other_core(theirs2), other_core(g2)
    ga, mine3 = together((ga, mine3))
    half = g.shape[0] // 2
    gc, gd = in_plane(ga[:half], 1, True), in_plane(gb[half:], -1, True)
    theirs3, ga2, gb2, mine4, passed1, passed2 = together(
        (theirs3, ga, gb, mine4, passed1, passed2)
    )
    passed3, gao, gbo = other_core(theirs3), other_core(ga2), other_core(gb2)
    gc, gd, mine4 = together((gc, gd, mine4))
    held = [tokens, mine1, mine2, mine3, mine4, passed1, passed2, passed3]
    return held, [g, ga, gb, gc, gd, go, gao, gbo, other_core(gc), other_core(gd)]


def high_low(v):
    high = v.astype(BF16).astype(F32)
    return high, (v - high).astype(BF16).astype(F32)


def shard_places(w_parts, sec):
    core = sec % CORES
    px = sec // (SIDE * CORES)
    py = (sec // CORES) % SIDE
    shards = []
    for mine in (True, False):
        group = w_parts[:5] if mine else w_parts[5:]
        col = core if mine else 1 - core
        for r2 in REACH:
            for at, r1 in enumerate(REACH):
                if r2 == 2:
                    ref, row = (group[3], at) if at < 2 else (group[4], at - 2)
                else:
                    ref, row = group[REACH.index(r2)], at
                dx = jnp.where(col == 0, r1, r2)
                dy = jnp.where(col == 0, r2, r1)
                s = (((px + dx + SIDE) % SIDE) * SIDE + (py + dy + SIDE) % SIDE) * CORES + col
                shards.append((ref, row, s))
    return shards


def attend_kernel(info, gains, *refs):
    x_parts, w_parts = refs[:8], refs[8:18]
    out, xs, ws, ks, vs, qs, scale, sems = refs[18:]
    sec, tp, first, own_a, own_b = (info[i] for i in range(5))
    turn = 2 * (sec % CORES) - 1
    for part, off in zip(x_parts, (0, 1, 2, 3, 4, -1, -2, -3)):
        at = pl.multiple_of(((tp + turn * off + 8) % 8) * 512, 512)
        pltpu.make_async_copy(part, xs.at[:, pl.ds(at, 512)], sems.at[0]).start()
    shards = shard_places(w_parts, sec)
    for kind in (2, 0, 1):
        for ref, row, s in shards:
            pltpu.make_async_copy(
                ref.at[pl.ds(row * 512 + kind * 128, 128)], ws.at[kind, s], sems.at[1 + kind]
            ).start()
    lane = lax.broadcasted_iota(jnp.int32, (1, 128), 1)
    rest = jnp.where(lane < 8, ABSENT, 0.0)
    out[:, :512] = jnp.zeros((512, 512), BF16)
    out[:, 512:] = jnp.broadcast_to(rest, (512, 128)).astype(BF16)

    pltpu.make_async_copy(xs, xs, sems.at[0]).wait()

    @pl.loop(0, 5)
    def _(i):
        rows = pl.ds(pl.multiple_of(i * 128, 128), 128)
        which = pl.ds((i == 4).astype(jnp.int32), 1)
        total = jnp.zeros((128, 1), F32)
        for j in range(8):
            cols = slice(512 * j, 512 * (j + 1))
            v = xs[rows, cols].astype(F32)
            total = total + jnp.sum(v * v, axis=1, keepdims=True)
            xs[rows, cols] = (v * gains[which, cols]).astype(BF16)
        scale[rows, :] = jnp.broadcast_to(lax.rsqrt(total / 4096.0 + 1e-06), (128, 128))

    for kind, rows, held in ((2, slice(512, 640), qs), (0, slice(0, 512), ks), (1, slice(0, 512), vs)):
        pltpu.make_async_copy(ws.at[kind], ws.at[kind], sems.at[1 + kind]).wait()

        @pl.loop(0, 2)
        def _(n):
            cols = pl.ds(pl.multiple_of(n * 256, 256), 256)
            part = ws[kind, :, :, cols].reshape(4096, 256)
            product = jnp.dot(xs[rows, :], part, preferred_element_type=F32)
            held[:, cols] = (product * scale[rows, 0:1]).astype(BF16)

    row_owner = first + lax.broadcasted_iota(jnp.int32, (128, 512), 0) // QTOK
    key_owner = jnp.where(lax.broadcasted_iota(jnp.int32, (128, 512), 1) < PTOK, own_a, own_b)
    keep = row_owner == key_owner
    window = pl.ds(pl.multiple_of(first * QTOK, QTOK), 128)
    lane = lax.broadcasted_iota(jnp.int32, (128, 128), 1)
    stats = jnp.zeros((128, 128), F32)
    for pair in range(4):
        cols = slice(128 * pair, 128 * (pair + 1))
        q2, k2, v2 = qs[:, cols], ks[:, cols], vs[:, cols]
        sums = []
        for side in range(2):
            h = 2 * pair + side
            mine = (lane < 64) if side == 0 else (lane >= 64)
            qh = jnp.where(mine, q2.astype(F32), 0.0).astype(BF16)
            scores = lax.dot_general(qh, k2, (((1,), (1,)), ((), ())), preferred_element_type=F32)
            scores = jnp.where(keep, scores, ABSENT)
            top_hi, top_lo = high_low(jnp.max(scores, axis=1, keepdims=True))
            weights = jnp.where(keep, jnp.exp(scores - (top_hi + top_lo)), 0.0)
            a_hi, a_lo = high_low(jnp.sum(weights[:, :PTOK], axis=1, keepdims=True))
            b_hi, b_lo = high_low(jnp.sum(weights[:, PTOK:], axis=1, keepdims=True))
            for at, value in enumerate((top_hi, top_lo, a_hi, a_lo, b_hi, b_lo)):
                stats = jnp.where(lane == 8 * at + h, value, stats)
            sums.append(jnp.dot(weights.astype(BF16), v2, preferred_element_type=F32))
        out[window, cols] = jnp.where(lane < 64, sums[0], sums[1]).astype(BF16)
    out[window, 512:640] = stats.astype(BF16)


def attend(info, gains, x_parts, w_parts):
    anywhere = pl.BlockSpec(memory_space=pl.ANY)
    inside = pl.BlockSpec(memory_space=pltpu.VMEM)
    return pl.pallas_call(
        attend_kernel,
        in_specs=[pl.BlockSpec(memory_space=pltpu.SMEM), inside] + [anywhere] * 18,
        out_specs=inside,
        out_shape=jax.ShapeDtypeStruct((512, 640), BF16),
        scratch_shapes=[
            pltpu.VMEM((640, 4096), BF16),
            pltpu.VMEM((3, 32, 128, 512), BF16),
            pltpu.VMEM((512, 512), BF16),
            pltpu.VMEM((512, 512), BF16),
            pltpu.VMEM((128, 512), BF16),
            pltpu.VMEM((640, 128), F32),
            pltpu.SemaphoreType.DMA((4,)),
        ],
        compiler_params=pltpu.CompilerParams(vmem_limit_bytes=58 * 2**20),
        cost_estimate=pl.CostEstimate(
            flops=5 * 10**9, bytes_accessed=30 * 2**20, transcendentals=2**19
        ),
        name="project_attend",
    )(info, gains, *x_parts, *w_parts)


def assemble_kernel(info, *refs):
    w_parts = refs[:10]
    wo, sem = refs[10:]
    for ref, row, s in shard_places(w_parts, info[0]):
        pltpu.make_async_copy(
            ref.at[pl.ds(row * 512 + 384, 128)],
            wo.at[pl.ds(pl.multiple_of(s * 128, 128), 128)],
            sem,
        ).start()
    pltpu.make_async_copy(wo, wo, sem).wait()


def assemble(info, w_parts):
    anywhere = pl.BlockSpec(memory_space=pl.ANY)
    return pl.pallas_call(
        assemble_kernel,
        in_specs=[pl.BlockSpec(memory_space=pltpu.SMEM)] + [anywhere] * 10,
        out_specs=pl.BlockSpec(memory_space=pltpu.VMEM),
        out_shape=jax.ShapeDtypeStruct((4096, 512), BF16),
        scratch_shapes=[pltpu.SemaphoreType.DMA(())],
        compiler_params=pltpu.CompilerParams(vmem_limit_bytes=58 * 2**20),
        cost_estimate=pl.CostEstimate(flops=0, bytes_accessed=8 * 2**20, transcendentals=0),
        name="assemble_out",
    )(info, *w_parts)


def merge_kernel(got, wo, out):
    st = got[:, 512:640].astype(F32)
    both = st + pltpu.roll(st, 120, 1)
    sum_a = pltpu.roll(both, 112, 1).reshape(32, 16, 128)
    sum_b = pltpu.roll(both, 96, 1).reshape(32, 16, 128)
    both = both.reshape(32, 16, 128)
    lane3 = lax.broadcasted_iota(jnp.int32, (32, 16, 128), 2)
    head = lane3 < 8
    tops = jnp.where(head, both, 0.0)
    top = jnp.max(tops, axis=0, keepdims=True)
    factor = jnp.exp(tops - top)
    sum_a = jnp.where(head, sum_a * factor, 0.0)
    sum_b = jnp.where(head, sum_b * factor, 0.0)
    total = jnp.sum(sum_a + sum_b, axis=0, keepdims=True)
    inverse = jnp.where(head[:1], 1.0 / total, 0.0)
    share_a = jnp.sum((sum_a * inverse).reshape(512, 128), axis=1, keepdims=True)
    share_b = jnp.sum((sum_b * inverse).reshape(512, 128), axis=1, keepdims=True)
    lane = lax.broadcasted_iota(jnp.int32, (512, 128), 1)
    slot = (lax.broadcasted_iota(jnp.int32, (512, 128), 0) // 16) * 2
    pooled = jnp.sum(
        jnp.where(lane == slot, share_a, 0.0) + jnp.where(lane == slot + 1, share_b, 0.0),
        axis=0,
        keepdims=True,
    )
    ratio_hi, ratio_lo = high_low((factor * inverse).reshape(512, 128))
    spread = (
        lax.broadcasted_iota(jnp.int32, (128, 512), 1) // HEAD_DIM
        == lax.broadcasted_iota(jnp.int32, (128, 512), 0)
    )
    spread = jnp.where(spread, 1.0, 0.0).astype(BF16)
    ratio = jnp.dot(ratio_hi.astype(BF16), spread, preferred_element_type=F32) + jnp.dot(
        ratio_lo.astype(BF16), spread, preferred_element_type=F32
    )
    context = jnp.sum((got[:, 0:512].astype(F32) * ratio).reshape(32, 16, 512), axis=0)
    context = context.astype(BF16)
    pool_hi, pool_lo = high_low(pooled)
    row = lax.broadcasted_iota(jnp.int32, (16, 128), 0)
    extra = jnp.where(row == 0, pool_hi, jnp.where(row == 1, pool_lo, 0.0)).astype(BF16)
    for z in range(8):
        term = lax.dot_general(
            context,
            wo[512 * z : 512 * (z + 1), :],
            (((1,), (1,)), ((), ())),
            preferred_element_type=F32,
        )
        out[z, :, 0:512] = term.astype(BF16)
        out[z, :, 512:640] = extra


def merge(got, wo):
    return pl.pallas_call(
        merge_kernel,
        out_shape=jax.ShapeDtypeStruct((8, 16, 640), BF16),
        compiler_params=pltpu.CompilerParams(vmem_limit_bytes=58 * 2**20),
        name="merge_project",
    )(got, wo)


def add_kernel(got, rows, out):
    sums = jnp.sum(got[...].astype(F32), axis=0)
    done = (rows[...].astype(F32) + sums[:, 0:512]).astype(BF16)
    pool_hi, pool_lo = high_low(jnp.sum(sums[:, 512:640], axis=0, keepdims=True))
    row = lax.broadcasted_iota(jnp.int32, (16, 128), 0)
    extra = jnp.where(row == 0, pool_hi, jnp.where(row == 1, pool_lo, 0.0)).astype(BF16)
    for s in range(32):
        out[s, :, 0:512] = done
        out[s, :, 512:640] = extra


def add_rows(got, rows):
    return pl.pallas_call(
        add_kernel,
        out_shape=jax.ShapeDtypeStruct((32, 16, 640), BF16),
        name="add_rows",
    )(got, rows)


def pack_kernel(
    info, encoded, states, w_key, w_value, w_query, w_out, gain_a, gain_b, tokens, shard, gains
):
    gains[0:1, :] = gain_a[...]
    gains[1:2, :] = gain_b[...]
    tokens[0:512, :] = encoded[...]
    tokens[512:640, :] = states[pl.ds(pl.multiple_of(info[2] * QTOK, QTOK), 2 * QTOK), :]
    shard[0:128, :] = w_key[...]
    shard[128:256, :] = w_value[...]
    shard[256:384, :] = w_query[...]
    shard[384:512, :] = w_out[...].T


def pack(info, *arrays):
    inside = pl.BlockSpec(memory_space=pltpu.VMEM)
    return pl.pallas_call(
        pack_kernel,
        in_specs=[pl.BlockSpec(memory_space=pltpu.SMEM)] + [inside] * 8,
        out_specs=[inside] * 3,
        out_shape=[
            jax.ShapeDtypeStruct((640, 512), BF16),
            jax.ShapeDtypeStruct((512, 512), BF16),
            jax.ShapeDtypeStruct((2, 4096), F32),
        ],
        name="pack",
    )(info, *arrays)


def on_device(
    encoded, decoder_states, passage_counts, enc_gain, dec_gain, w_key, w_value, w_query, w_out
):
    sec = lax.axis_index("sec")
    tp = lax.axis_index("tp")
    questions = decoder_states.shape[0] // QTOK
    order = jnp.arange(questions, dtype=jnp.int32)
    ends = jnp.sum(jnp.where(order[:, None] <= order[None, :], passage_counts[:, None], 0), axis=0)
    slots = sec * 2 + jnp.arange(2, dtype=jnp.int32)
    owner = jnp.sum((slots[:, None] >= ends[None, :]).astype(jnp.int32), axis=1)
    first = jnp.minimum(owner[0], questions - 2)
    info = jnp.stack([sec, tp, first, owner[0], owner[1]]).astype(jnp.int32)
    tokens, shard, gains = pack(
        info,
        encoded,
        decoder_states,
        w_key,
        w_value,
        w_query,
        w_out,
        enc_gain.reshape(1, -1),
        dec_gain.reshape(1, -1),
    )
    x_parts, w_parts = gather(tokens, shard)
    partial = attend(info, gains, x_parts, w_parts)
    got = lax.all_to_all(partial, "sec", 0, 0, tiled=True)
    terms = merge(got, assemble(info, w_parts))
    terms = lax.all_to_all(terms, "tp", 0, 0, tiled=True)
    rows = lax.dynamic_slice_in_dim(decoder_states, sec * 16, 16, 0)
    finished = lax.all_to_all(add_rows(terms, rows), "sec", 0, 0, tiled=True)
    decoded = finished[:, :, 0:512].reshape(512, 512)
    pooled = jnp.sum(finished[:, 0:2, 512:640].astype(F32), axis=(0, 1))
    passage_scores = lax.dynamic_slice_in_dim(pooled, sec * 2, 2, 0) / (HEADS * QTOK)
    return (decoded, passage_scores)


def solution(mesh):
    placed = (
        P("sec", "tp"),
        P(None, "tp"),
        P(),
        P(),
        P(),
        P("sec", "tp"),
        P("sec", "tp"),
        P("sec", "tp"),
        P("tp", "sec"),
    )
    return jax.shard_map(
        on_device, mesh=mesh, in_specs=placed, out_specs=(P(None, "tp"), P("sec")), check_vma=False
    )
```

```python
import jax
import jax.numpy as jnp
from jax import lax
from jax.experimental import pallas as pl
from jax.experimental.pallas import tpu as pltpu
from jax.sharding import PartitionSpec as P

HEADS = 64
HEAD_DIM = 64
PTOK = 256
QTOK = 64
SIDE = 4
CORES = 2
ABSENT = -1e30
BF16 = jnp.bfloat16
F32 = jnp.float32
REACH = (0, -1, 1, 2)


def sec_id(x, y, c):
    return ((x % SIDE) * SIDE + y % SIDE) * CORES + c


def along_tp(v, step):
    n = lax.axis_size("tp")
    return lax.ppermute(v, "tp", [(i, (i + step) % n) for i in range(n)])


def along_tp_by_core(v):
    n = lax.axis_size("tp")
    s = lax.axis_size("sec")
    pairs = [
        (i * n + z, i * n + (z + (1 if i % CORES == 0 else -1)) % n)
        for i in range(s)
        for z in range(n)
    ]
    return lax.ppermute(v, ("sec", "tp"), pairs)


def other_core(v):
    s = lax.axis_size("sec")
    return lax.ppermute(v, "sec", [(i, i ^ 1) for i in range(s)])


def in_plane(v, step, swap):
    pairs = []
    for x in range(SIDE):
        for y in range(SIDE):
            for c in range(CORES):
                on_x = (c == 0) != swap
                to = sec_id(x + step, y, c) if on_x else sec_id(x, y + step, c)
                pairs.append((sec_id(x, y, c), to))
    return lax.ppermute(v, "sec", pairs)


def gather(tokens, shard):
    together = lax.optimization_barrier
    half = shard.shape[0] // 2
    theirs = other_core(tokens)
    mine1, theirs1 = along_tp_by_core(tokens), along_tp_by_core(theirs)
    a, b = in_plane(shard, 1, False), in_plane(shard, -1, False)
    a, b, mine1 = together((a, b, mine1))
    c, d = in_plane(a[:half], 1, False), in_plane(b[half:], -1, False)
    mine2 = along_tp_by_core(mine1)
    c, d, theirs1 = together((c, d, theirs1))
    theirs2 = along_tp_by_core(theirs1)
    g = jnp.concatenate([shard, a, b, c, d], 0)
    g2, mine2 = together((g, mine2))
    ga, gb = in_plane(g, 1, True), in_plane(g2, -1, True)
    mine3 = along_tp_by_core(mine2)
    passed1 = other_core(theirs1)
    theirs3 = along_tp_by_core(theirs2)
    mine4 = along_tp_by_core(mine3)
    passed2, go = other_core(theirs2), other_core(g2)
    ga, mine3 = together((ga, mine3))
    half = g.shape[0] // 2
    gc, gd = in_plane(ga[:half], 1, True), in_plane(gb[half:], -1, True)
    theirs3, ga2, gb2, mine4, passed1, passed2 = together(
        (theirs3, ga, gb, mine4, passed1, passed2)
    )
    passed3, gao, gbo = other_core(theirs3), other_core(ga2), other_core(gb2)
    gc, gd, mine4 = together((gc, gd, mine4))
    held = [tokens, mine1, mine2, mine3, mine4, passed1, passed2, passed3]
    return held, [g, ga, gb, gc, gd, go, gao, gbo, other_core(gc), other_core(gd)]


def high_low(v):
    high = v.astype(BF16).astype(F32)
    return high, (v - high).astype(BF16).astype(F32)


def shard_places(w_parts, sec):
    core = sec % CORES
    px = sec // (SIDE * CORES)
    py = (sec // CORES) % SIDE
    shards = []
    for mine in (True, False):
        group = w_parts[:5] if mine else w_parts[5:]
        col = core if mine else 1 - core
        for r2 in REACH:
            for at, r1 in enumerate(REACH):
                if r2 == 2:
                    ref, row = (group[3], at) if at < 2 else (group[4], at - 2)
                else:
                    ref, row = group[REACH.index(r2)], at
                dx = jnp.where(col == 0, r1, r2)
                dy = jnp.where(col == 0, r2, r1)
                s = (((px + dx + SIDE) % SIDE) * SIDE + (py + dy + SIDE) % SIDE) * CORES + col
                shards.append((ref, row, s))
    return shards


def attend_kernel(info, gains, *refs):
    x_parts, w_parts = refs[:8], refs[8:18]
    out, xs, ws, ks, vs, qs, scale, sems = refs[18:]
    sec, tp, first, own_a, own_b = (info[i] for i in range(5))
    turn = 2 * (sec % CORES) - 1
    for part, off in zip(x_parts, (0, 1, 2, 3, 4, -1, -2, -3)):
        at = pl.multiple_of(((tp + turn * off + 8) % 8) * 512, 512)
        pltpu.make_async_copy(part, xs.at[:, pl.ds(at, 512)], sems.at[0]).start()
    shards = shard_places(w_parts, sec)
    for kind in (2, 0, 1):
        for ref, row, s in shards:
            pltpu.make_async_copy(
                ref.at[pl.ds(row * 512 + kind * 128, 128)], ws.at[kind, s], sems.at[1 + kind]
            ).start()
    lane = lax.broadcasted_iota(jnp.int32, (1, 128), 1)
    rest = jnp.where(lane < 8, ABSENT, 0.0)
    out[:, :512] = jnp.zeros((512, 512), BF16)
    out[:, 512:] = jnp.broadcast_to(rest, (512, 128)).astype(BF16)

    pltpu.make_async_copy(xs, xs, sems.at[0]).wait()

    @pl.loop(0, 5)
    def _(i):
        rows = pl.ds(pl.multiple_of(i * 128, 128), 128)
        which = pl.ds((i == 4).astype(jnp.int32), 1)
        total = jnp.zeros((128, 1), F32)
        for j in range(8):
            cols = slice(512 * j, 512 * (j + 1))
            v = xs[rows, cols].astype(F32)
            total = total + jnp.sum(v * v, axis=1, keepdims=True)
            xs[rows, cols] = (v * gains[which, cols]).astype(BF16)
        scale[rows, :] = jnp.broadcast_to(lax.rsqrt(total / 4096.0 + 1e-06), (128, 128))

    for kind, rows, held in ((2, slice(512, 640), qs), (0, slice(0, 512), ks), (1, slice(0, 512), vs)):
        pltpu.make_async_copy(ws.at[kind], ws.at[kind], sems.at[1 + kind]).wait()

        @pl.loop(0, 2)
        def _(n):
            cols = pl.ds(pl.multiple_of(n * 256, 256), 256)
            part = ws[kind, :, :, cols].reshape(4096, 256)
            product = jnp.dot(xs[rows, :], part, preferred_element_type=F32)
            held[:, cols] = (product * scale[rows, 0:1]).astype(BF16)

    row_owner = first + lax.broadcasted_iota(jnp.int32, (128, 512), 0) // QTOK
    key_owner = jnp.where(lax.broadcasted_iota(jnp.int32, (128, 512), 1) < PTOK, own_a, own_b)
    keep = row_owner == key_owner
    window = pl.ds(pl.multiple_of(first * QTOK, QTOK), 128)
    lane = lax.broadcasted_iota(jnp.int32, (128, 128), 1)
    stats = jnp.zeros((128, 128), F32)
    for pair in range(4):
        cols = slice(128 * pair, 128 * (pair + 1))
        q2, k2, v2 = qs[:, cols], ks[:, cols], vs[:, cols]
        sums = []
        for side in range(2):
            h = 2 * pair + side
            mine = (lane < 64) if side == 0 else (lane >= 64)
            qh = jnp.where(mine, q2.astype(F32), 0.0).astype(BF16)
            scores = lax.dot_general(qh, k2, (((1,), (1,)), ((), ())), preferred_element_type=F32)
            scores = jnp.where(keep, scores, ABSENT)
            top_hi, top_lo = high_low(jnp.max(scores, axis=1, keepdims=True))
            weights = jnp.where(keep, jnp.exp(scores - (top_hi + top_lo)), 0.0)
            a_hi, a_lo = high_low(jnp.sum(weights[:, :PTOK], axis=1, keepdims=True))
            b_hi, b_lo = high_low(jnp.sum(weights[:, PTOK:], axis=1, keepdims=True))
            for at, value in enumerate((top_hi, top_lo, a_hi, a_lo, b_hi, b_lo)):
                stats = jnp.where(lane == 8 * at + h, value, stats)
            sums.append(jnp.dot(weights.astype(BF16), v2, preferred_element_type=F32))
        out[window, cols] = jnp.where(lane < 64, sums[0], sums[1]).astype(BF16)
    out[window, 512:640] = stats.astype(BF16)


def attend(info, gains, x_parts, w_parts):
    anywhere = pl.BlockSpec(memory_space=pl.ANY)
    inside = pl.BlockSpec(memory_space=pltpu.VMEM)
    return pl.pallas_call(
        attend_kernel,
        in_specs=[pl.BlockSpec(memory_space=pltpu.SMEM), inside] + [anywhere] * 18,
        out_specs=inside,
        out_shape=jax.ShapeDtypeStruct((512, 640), BF16),
        scratch_shapes=[
            pltpu.VMEM((640, 4096), BF16),
            pltpu.VMEM((3, 32, 128, 512), BF16),
            pltpu.VMEM((512, 512), BF16),
            pltpu.VMEM((512, 512), BF16),
            pltpu.VMEM((128, 512), BF16),
            pltpu.VMEM((640, 128), F32),
            pltpu.SemaphoreType.DMA((4,)),
        ],
        compiler_params=pltpu.CompilerParams(vmem_limit_bytes=58 * 2**20),
        cost_estimate=pl.CostEstimate(
            flops=5 * 10**9, bytes_accessed=30 * 2**20, transcendentals=2**19
        ),
        name="project_attend",
    )(info, gains, *x_parts, *w_parts)


def assemble_kernel(info, *refs):
    w_parts = refs[:10]
    wo, sem = refs[10:]
    for ref, row, s in shard_places(w_parts, info[0]):
        pltpu.make_async_copy(
            ref.at[pl.ds(row * 512 + 384, 128)],
            wo.at[pl.ds(pl.multiple_of(s * 128, 128), 128)],
            sem,
        ).start()
    pltpu.make_async_copy(wo, wo, sem).wait()


def assemble(info, w_parts):
    anywhere = pl.BlockSpec(memory_space=pl.ANY)
    return pl.pallas_call(
        assemble_kernel,
        in_specs=[pl.BlockSpec(memory_space=pltpu.SMEM)] + [anywhere] * 10,
        out_specs=pl.BlockSpec(memory_space=pltpu.VMEM),
        out_shape=jax.ShapeDtypeStruct((4096, 512), BF16),
        scratch_shapes=[pltpu.SemaphoreType.DMA(())],
        compiler_params=pltpu.CompilerParams(vmem_limit_bytes=58 * 2**20),
        cost_estimate=pl.CostEstimate(flops=0, bytes_accessed=8 * 2**20, transcendentals=0),
        name="assemble_out",
    )(info, *w_parts)


def merge_kernel(got, rows, out, wo, sems):
    for z in range(8):
        at = pl.ds(512 * z, 512)
        pltpu.make_async_copy(rows.at[at], wo.at[at], sems.at[z]).start()
    st = got[:, 512:640].astype(F32)
    both = st + pltpu.roll(st, 120, 1)
    sum_a = pltpu.roll(both, 112, 1).reshape(32, 16, 128)
    sum_b = pltpu.roll(both, 96, 1).reshape(32, 16, 128)
    both = both.reshape(32, 16, 128)
    lane3 = lax.broadcasted_iota(jnp.int32, (32, 16, 128), 2)
    head = lane3 < 8
    tops = jnp.where(head, both, 0.0)
    top = jnp.max(tops, axis=0, keepdims=True)
    factor = jnp.exp(tops - top)
    sum_a = jnp.where(head, sum_a * factor, 0.0)
    sum_b = jnp.where(head, sum_b * factor, 0.0)
    total = jnp.sum(sum_a + sum_b, axis=0, keepdims=True)
    inverse = jnp.where(head[:1], 1.0 / total, 0.0)
    share_a = jnp.sum((sum_a * inverse).reshape(512, 128), axis=1, keepdims=True)
    share_b = jnp.sum((sum_b * inverse).reshape(512, 128), axis=1, keepdims=True)
    lane = lax.broadcasted_iota(jnp.int32, (512, 128), 1)
    slot = (lax.broadcasted_iota(jnp.int32, (512, 128), 0) // 16) * 2
    pooled = jnp.sum(
        jnp.where(lane == slot, share_a, 0.0) + jnp.where(lane == slot + 1, share_b, 0.0),
        axis=0,
        keepdims=True,
    )
    ratio_hi, ratio_lo = high_low((factor * inverse).reshape(512, 128))
    spread = (
        lax.broadcasted_iota(jnp.int32, (128, 512), 1) // HEAD_DIM
        == lax.broadcasted_iota(jnp.int32, (128, 512), 0)
    )
    spread = jnp.where(spread, 1.0, 0.0).astype(BF16)
    ratio = jnp.dot(ratio_hi.astype(BF16), spread, preferred_element_type=F32) + jnp.dot(
        ratio_lo.astype(BF16), spread, preferred_element_type=F32
    )
    context = jnp.sum((got[:, 0:512].astype(F32) * ratio).reshape(32, 16, 512), axis=0)
    context = context.astype(BF16)
    pool_hi, pool_lo = high_low(pooled)
    row = lax.broadcasted_iota(jnp.int32, (16, 128), 0)
    extra = jnp.where(row == 0, pool_hi, jnp.where(row == 1, pool_lo, 0.0)).astype(BF16)
    for z in range(8):
        at = pl.ds(512 * z, 512)
        pltpu.make_async_copy(rows.at[at], wo.at[at], sems.at[z]).wait()
        term = lax.dot_general(
            context,
            wo[512 * z : 512 * (z + 1), :],
            (((1,), (1,)), ((), ())),
            preferred_element_type=F32,
        )
        out[z, :, 0:512] = term.astype(BF16)
        out[z, :, 512:640] = extra


def merge(got, wo):
    return pl.pallas_call(
        merge_kernel,
        in_specs=[
            pl.BlockSpec(memory_space=pltpu.VMEM),
            pl.BlockSpec(memory_space=pl.ANY),
        ],
        out_specs=pl.BlockSpec(memory_space=pltpu.VMEM),
        out_shape=jax.ShapeDtypeStruct((8, 16, 640), BF16),
        scratch_shapes=[pltpu.VMEM((4096, 512), BF16), pltpu.SemaphoreType.DMA((8,))],
        compiler_params=pltpu.CompilerParams(vmem_limit_bytes=58 * 2**20),
        name="merge_project",
    )(got, wo)


def add_kernel(got, rows, out):
    sums = jnp.sum(got[...].astype(F32), axis=0)
    done = (rows[...].astype(F32) + sums[:, 0:512]).astype(BF16)
    pool_hi, pool_lo = high_low(jnp.sum(sums[:, 512:640], axis=0, keepdims=True))
    row = lax.broadcasted_iota(jnp.int32, (16, 128), 0)
    extra = jnp.where(row == 0, pool_hi, jnp.where(row == 1, pool_lo, 0.0)).astype(BF16)
    for s in range(32):
        out[s, :, 0:512] = done
        out[s, :, 512:640] = extra


def add_rows(got, rows):
    return pl.pallas_call(
        add_kernel,
        out_shape=jax.ShapeDtypeStruct((32, 16, 640), BF16),
        name="add_rows",
    )(got, rows)


def pack_kernel(
    info, encoded, states, w_key, w_value, w_query, w_out, gain_a, gain_b, tokens, shard, gains
):
    gains[0:1, :] = gain_a[...]
    gains[1:2, :] = gain_b[...]
    tokens[0:512, :] = encoded[...]
    tokens[512:640, :] = states[pl.ds(pl.multiple_of(info[2] * QTOK, QTOK), 2 * QTOK), :]
    shard[0:128, :] = w_key[...]
    shard[128:256, :] = w_value[...]
    shard[256:384, :] = w_query[...]
    shard[384:512, :] = w_out[...].T


def pack(info, *arrays):
    inside = pl.BlockSpec(memory_space=pltpu.VMEM)
    return pl.pallas_call(
        pack_kernel,
        in_specs=[pl.BlockSpec(memory_space=pltpu.SMEM)] + [inside] * 8,
        out_specs=[inside] * 3,
        out_shape=[
            jax.ShapeDtypeStruct((640, 512), BF16),
            jax.ShapeDtypeStruct((512, 512), BF16),
            jax.ShapeDtypeStruct((2, 4096), F32),
        ],
        name="pack",
    )(info, *arrays)


def on_device(
    encoded, decoder_states, passage_counts, enc_gain, dec_gain, w_key, w_value, w_query, w_out
):
    sec = lax.axis_index("sec")
    tp = lax.axis_index("tp")
    questions = decoder_states.shape[0] // QTOK
    order = jnp.arange(questions, dtype=jnp.int32)
    ends = jnp.sum(jnp.where(order[:, None] <= order[None, :], passage_counts[:, None], 0), axis=0)
    slots = sec * 2 + jnp.arange(2, dtype=jnp.int32)
    owner = jnp.sum((slots[:, None] >= ends[None, :]).astype(jnp.int32), axis=1)
    first = jnp.minimum(owner[0], questions - 2)
    info = jnp.stack([sec, tp, first, owner[0], owner[1]]).astype(jnp.int32)
    tokens, shard, gains = pack(
        info,
        encoded,
        decoder_states,
        w_key,
        w_value,
        w_query,
        w_out,
        enc_gain.reshape(1, -1),
        dec_gain.reshape(1, -1),
    )
    x_parts, w_parts = gather(tokens, shard)
    partial = attend(info, gains, x_parts, w_parts)
    got = lax.all_to_all(partial, "sec", 0, 0, tiled=True)
    terms = merge(got, assemble(info, w_parts))
    terms = lax.all_to_all(terms, "tp", 0, 0, tiled=True)
    rows = lax.dynamic_slice_in_dim(decoder_states, sec * 16, 16, 0)
    finished = lax.all_to_all(add_rows(terms, rows), "sec", 0, 0, tiled=True)
    decoded = finished[:, :, 0:512].reshape(512, 512)
    pooled = jnp.sum(finished[:, 0:2, 512:640].astype(F32), axis=(0, 1))
    passage_scores = lax.dynamic_slice_in_dim(pooled, sec * 2, 2, 0) / (HEADS * QTOK)
    return (decoded, passage_scores)


def solution(mesh):
    placed = (
        P("sec", "tp"),
        P(None, "tp"),
        P(),
        P(),
        P(),
        P("sec", "tp"),
        P("sec", "tp"),
        P("sec", "tp"),
        P("tp", "sec"),
    )
    return jax.shard_map(
        on_device, mesh=mesh, in_specs=placed, out_specs=(P(None, "tp"), P("sec")), check_vma=False
    )
```
